512 devices in a mesh: row: 32 (over x, z), col: 16 (over y, core).
Axes of the slice: x: 4, y: 8, z: 8, core: 2. Of those that a mesh axis runs over, the one named last changes fastest.
Arguments:
- node_coords: int32 [3, 65536], P(None, ('row', 'col')), may hold values from 0 to 1023
- inv_range: float32 [3], replicated, may hold values from 0.008 to 0.03
- mode_block: float32 [96, 65536], P(None, ('row', 'col')), may hold values from -40 to 40
Outputs:
- basis: float32 [96, 65536], P(None, ('row', 'col'))
- ritz: float32 [96, 96], replicated
The draws below stay inside these ranges and needn't reach their ends.
All inputs are finite; a program needn't handle non-finite values.
Results may differ from the reference program's by a relative error of at most 0.00055.
The reference program's roundings to bfloat16 on the way (of `low_modes` and `covariance`) count: a program that leaves them out, or rounds other values in their place, can miss the bound.
Values may be sent and summed in bfloat16 or wider, within the bound.
No kernel may reach another device: no remote copies, remote signals or barrier semaphores. Data moves between devices by JAX's collectives and lax.ppermute only.
A program may use at most 64 MiB of HBM per device.

```python
import math
import jax
import jax.numpy as jnp
from jax import lax

MODES = 96
SPAN = 1024
NODES = 65536


def draw_mode_block(key, part):
    key_scale, key_nodes, key_values = jax.random.split(key, 3)
    mode_scale = jnp.exp(jax.random.uniform(key_scale, (MODES, 1), jnp.float32, math.log(0.3), math.log(3.0)))
    node_noise = jnp.exp(jax.random.uniform(key_nodes, (1, NODES), jnp.float32, math.log(0.55), math.log(1.8)))
    node_place = jnp.arange(NODES, dtype=jnp.float32) / (NODES - 1)
    trend = jnp.exp((node_place - 0.5) * math.log(3.0))
    values = jax.random.truncated_normal(key_values, -4.0, 4.0, (MODES, NODES), jnp.float32)
    return (values * mode_scale * trend[None, :] * node_noise).astype(jnp.float32)


def with_ends(result, own_key, low, top_value):
    dims = result.shape
    index_at = [jax.random.randint(jax.random.fold_in(own_key, axis), (), 0, dims[axis]) for axis in range(len(dims))]
    result = result.at[tuple(index_at)].set(low)
    longest = dims.index(max(dims))
    index_at[longest] = (index_at[longest] + 1) % dims[longest]
    return result.at[tuple(index_at)].set(top_value)


def setup_inputs(seed: int = 0) -> dict:
    keys = jax.random.split(jax.random.key(seed), 4)
    node_coords = with_ends(jax.random.randint(keys[0], (3, NODES), 0, SPAN), jax.random.fold_in(keys[0], 1), 0, SPAN - 1).astype(jnp.int32)
    inv_range = jnp.clip(jnp.exp(jax.random.uniform(keys[1], (3,), jnp.float32, math.log(0.008), math.log(0.03))), 0.008, 0.03)
    mode_block = draw_mode_block(jax.random.fold_in(keys[3], 71), 0)
    return {"node_coords": node_coords, "inv_range": inv_range, "mode_block": mode_block}


NUGGET = 0.25

def covariance(row_parts, col_parts, inv_range):
    diff = row_parts - col_parts
    delta_x = diff[0].astype(jnp.float32) * inv_range[0]
    delta_y = diff[1].astype(jnp.float32) * inv_range[1]
    delta_z = diff[2].astype(jnp.float32) * inv_range[2]
    squared = delta_x * delta_x + delta_y * delta_y + delta_z * delta_z
    return jnp.exp(1.0 - jnp.sqrt(1.0 + squared)).astype(jnp.bfloat16)

def reference(node_coords, inv_range, mode_block):
    mode_count = mode_block.shape[0]
    node_total = mode_block.shape[1]
    block_rows = math.gcd(node_total, 256)
    low_modes = mode_block.astype(jnp.bfloat16)
    row_blocks = node_coords.reshape(3, node_total // block_rows, block_rows).transpose(1, 0, 2)

    def one_block(block_pts):
        kernel = covariance(block_pts[:, :, None], node_coords[:, None, :], inv_range)
        return jnp.dot(low_modes.astype(jnp.float32), kernel.T.astype(jnp.float32), preferred_element_type=jnp.float32)
    pieces = lax.map(one_block, row_blocks)
    power_image = pieces.transpose(1, 0, 2).reshape(mode_count, node_total) + NUGGET * mode_block
    image_gram = jnp.dot(power_image, power_image.T, precision=lax.Precision.HIGHEST) / node_total
    lower = jnp.linalg.cholesky(image_gram)
    basis = jax.scipy.linalg.solve_triangular(lower, power_image, lower=True)
    mode_gram = jnp.dot(mode_block, mode_block.T, precision=lax.Precision.HIGHEST) / node_total
    cross = jnp.dot(mode_block, power_image.T, precision=lax.Precision.HIGHEST) / node_total
    lower_modes = jnp.linalg.cholesky(mode_gram)
    half_solved = jax.scipy.linalg.solve_triangular(lower_modes, cross, lower=True)
    ritz = jax.scipy.linalg.solve_triangular(lower_modes, half_solved.T, lower=True).T
    return (basis, ritz)
```

```python
import functools
import math

import jax
import jax.numpy as jnp
from jax import lax
from jax.experimental import pallas as pl
from jax.experimental.pallas import tpu as pltpu
from jax.sharding import Mesh, PartitionSpec as P

NUGGET = 0.25
LOG2E = math.log2(math.e)
CENTRE = 512.0
HIGHEST = lax.Precision.HIGHEST
PARAMS = pltpu.CompilerParams(vmem_limit_bytes=48 * 1024 * 1024)


def scaled_coords(pack, scale):
    parts = pack.astype(jnp.float32)
    return (parts[0:8] * 4.0 + (parts[8:16] - CENTRE)) * scale


def scale_rows(range_ref):
    index = lax.broadcasted_iota(jnp.int32, (8, 128), 0)
    picked = jnp.where(
        index == 0,
        range_ref[0],
        jnp.where(index == 1, range_ref[1], jnp.where(index == 2, range_ref[2], 0.0)),
    )
    return picked * LOG2E


def cov_kernel(first, modes, range_ref, row_ref, col_ref, *refs):
    if first:
        out_ref, rows, cols = refs
    else:
        start_ref, out_ref, rows, cols = refs
    pieces, _, width = col_ref.shape
    dests = row_ref.shape[0]
    scale = scale_rows(range_ref)
    for y in range(dests):
        rows[:, y * width : (y + 1) * width] = scaled_coords(row_ref[y], scale)
    if first:
        out_ref[...] = jnp.zeros_like(out_ref)
    else:
        out_ref[...] = start_ref[...]

    @pl.loop(0, pieces // 2)
    def _(step):
        low = []
        for half in range(2):
            piece = step * 2 + half
            low.append(col_ref[piece, 0:modes, :])
            coords = scaled_coords(col_ref[piece, modes : modes + 16, :], scale)
            cols[half * width : (half + 1) * width, :] = coords.T
        low = jnp.concatenate(low, axis=1)
        for pair in range(dests // 2):
            total = LOG2E * LOG2E
            for d in range(3):
                delta = cols[:, d : d + 1] - rows[d : d + 1, pair * 2 * width : (pair + 1) * 2 * width]
                total = total + delta * delta
            cov = jnp.exp2(LOG2E - total * lax.rsqrt(total)).astype(jnp.bfloat16)
            update = jnp.dot(low, cov, preferred_element_type=jnp.float32)
            out_ref[2 * pair] += update[:, :width]
            out_ref[2 * pair + 1] += update[:, width:]


def covariance_part(inv_range, row_pack, col_pack, start=None):
    dests, _, width = row_pack.shape
    modes = col_pack.shape[1] - 16
    pairs = col_pack.shape[0] * dests * width * width
    vmem = pl.BlockSpec(memory_space=pltpu.VMEM)
    args = (inv_range, row_pack, col_pack) + (() if start is None else (start,))
    return pl.pallas_call(
        functools.partial(cov_kernel, start is None, modes),
        out_shape=jax.ShapeDtypeStruct((dests, modes, width), jnp.float32),
        in_specs=[pl.BlockSpec(memory_space=pltpu.SMEM)] + [vmem] * (len(args) - 1),
        out_specs=vmem,
        scratch_shapes=[
            pltpu.VMEM((8, dests * width), jnp.float32),
            pltpu.VMEM((2 * width, 8), jnp.float32),
        ],
        compiler_params=PARAMS,
        cost_estimate=pl.CostEstimate(
            flops=pairs * (2 * modes + 12), bytes_accessed=4 * dests * modes * width, transcendentals=2 * pairs
        ),
    )(*args)


def nt_dot(left, right):
    return lax.dot_general(
        left, right, (((1,), (1,)), ((), ())), precision=HIGHEST, preferred_element_type=jnp.float32
    )


def gram_kernel(part_ref, mode_ref, image_ref, gram_ref):
    image = part_ref[0]
    for y in range(1, part_ref.shape[0]):
        image = image + part_ref[y]
    mode = mode_ref[...]
    image = image + NUGGET * mode
    image_ref[...] = image
    modes = image.shape[0]
    tiles = modes // 8
    slots = gram_ref.shape[0]
    grams = (nt_dot(image, image), nt_dot(mode, image), nt_dot(mode, mode))
    gram_ref[...] = jnp.zeros_like(gram_ref)
    for which, gram in enumerate(grams):
        for t in range(tiles):
            place = which * tiles + t
            slot, level = place % slots, place // slots
            gram_ref[slot, level * 8 : level * 8 + 8, 0:modes] = gram[t * 8 : t * 8 + 8, :]


def spread_kernel(part_ref, out_ref):
    total = part_ref[0]
    for k in range(1, part_ref.shape[0]):
        total = total + part_ref[k]
    for k in range(out_ref.shape[0]):
        out_ref[k] = total


def final_kernel(node_total, gram_ref, image_ref, basis_ref, ritz_ref):
    modes, width = image_ref.shape
    tiles = modes // 8
    slots = gram_ref.shape[0]

    def tile(which, t):
        place = which * tiles + t
        slot, level = place % slots, place // slots
        return gram_ref[slot, level * 8 : level * 8 + 8, :] * (1.0 / node_total)

    lane = lax.broadcasted_iota(jnp.int32, (8, width), 1)
    row = lax.broadcasted_iota(jnp.int32, (8, width), 0)
    left = [[tile(0, t) for t in range(tiles)], [tile(2, t) for t in range(tiles)]]
    right = [
        [image_ref[t * 8 : t * 8 + 8, :] for t in range(tiles)],
        [jnp.where(lane == row + 8 * t, 1.0, 0.0) for t in range(tiles)],
    ]
    for k in range(modes):
        home, sub = divmod(k, 8)
        for m in range(2):
            a, b = left[m], right[m]
            spread = {t: jnp.broadcast_to(a[t][:, k : k + 1], (8, width)) for t in range(home, tiles)}
            inverse = 1.0 / spread[home][sub : sub + 1, :]
            row_a = jnp.broadcast_to(a[home][sub : sub + 1, :] * inverse, (8, width))
            row_b = jnp.broadcast_to(b[home][sub : sub + 1, :] * inverse, (8, width))
            for t in range(home, tiles):
                factor = spread[t]
                if t == home:
                    if sub == 7:
                        continue
                    factor = jnp.where(row > sub, factor, 0.0)
                a[t] = a[t] - factor * row_a
                b[t] = b[t] - factor * row_b

    def finish(m):
        rows = []
        for t in range(tiles):
            pivot = jnp.sum(jnp.where(lane == row + 8 * t, left[m][t], 0.0), axis=1, keepdims=True)
            rows.append(right[m][t] * (1.0 / jnp.sqrt(pivot)))
        return jnp.concatenate(rows, axis=0)

    basis_ref[...] = finish(0)
    inverse = finish(1)[:, 0:modes]
    cross = jnp.concatenate([tile(1, t) for t in range(tiles)], axis=0)[:, 0:modes]
    half = jnp.dot(inverse, cross, precision=HIGHEST, preferred_element_type=jnp.float32)
    ritz_ref[...] = nt_dot(half, inverse)


def call(kernel, out_shape, *args):
    return pl.pallas_call(kernel, out_shape=out_shape, compiler_params=PARAMS)(*args)


def body(node_coords, inv_range, mode_block):
    modes, width = mode_block.shape
    groups, stripes, cores = lax.axis_size("row"), lax.axis_size("y"), lax.axis_size("c")
    node_total = groups * stripes * cores * width
    low = mode_block.astype(jnp.bfloat16)
    blank = jnp.zeros((5, width), jnp.bfloat16)
    coords = jnp.concatenate(
        [(node_coords // 4).astype(jnp.bfloat16), blank, (node_coords % 4).astype(jnp.bfloat16), blank], axis=0
    )
    pack = jnp.concatenate([low, coords], axis=0)
    own = lax.all_to_all(jnp.broadcast_to(pack[None], (groups,) + pack.shape), "row", 0, 0)
    row_pack = lax.all_to_all(jnp.broadcast_to(coords[None], (stripes,) + coords.shape), "y", 0, 0)
    sibling = lax.ppermute(own, "c", [(0, 1), (1, 0)])
    partial = covariance_part(inv_range, row_pack, own)
    partial = covariance_part(inv_range, row_pack, sibling, partial)
    pieces = lax.all_to_all(partial, "y", 0, 0)
    slots = stripes * cores
    levels = -(-3 * (modes // 8) // slots)
    image, grams = call(
        gram_kernel,
        (
            jax.ShapeDtypeStruct((modes, width), jnp.float32),
            jax.ShapeDtypeStruct((slots, 8 * levels, 128), jnp.float32),
        ),
        pieces,
        mode_block,
    )
    grams = lax.all_to_all(grams, ("y", "c"), 0, 0)
    grams = call(spread_kernel, jax.ShapeDtypeStruct((groups, 8 * levels, 128), jnp.float32), grams)
    grams = lax.all_to_all(grams, "row", 0, 0)
    grams = call(spread_kernel, jax.ShapeDtypeStruct((slots, 8 * levels, 128), jnp.float32), grams)
    grams = lax.all_to_all(grams, ("y", "c"), 0, 0)
    basis, ritz = call(
        functools.partial(final_kernel, node_total),
        (
            jax.ShapeDtypeStruct((modes, width), jnp.float32),
            jax.ShapeDtypeStruct((modes, modes), jnp.float32),
        ),
        grams,
        image,
    )
    return (basis, ritz)


def solution(mesh):
    groups, slots = mesh.devices.shape
    parts = Mesh(mesh.devices.reshape(groups, slots // 2, 2), ("row", "y", "c"))
    nodes = P(None, ("row", "y", "c"))
    return jax.shard_map(
        body, mesh=parts, in_specs=(nodes, P(), nodes), out_specs=(nodes, P()), check_vma=False
    )
```

```python
import functools
import math

import jax
import jax.numpy as jnp
from jax import lax
from jax.experimental import pallas as pl
from jax.experimental.pallas import tpu as pltpu
from jax.sharding import Mesh, PartitionSpec as P

NUGGET = 0.25
LOG2E = math.log2(math.e)
CENTRE = 512.0
HIGHEST = lax.Precision.HIGHEST
PARAMS = pltpu.CompilerParams(vmem_limit_bytes=48 * 1024 * 1024)


def scaled_coords(pack, scale):
    parts = pack.astype(jnp.float32)
    return (parts[0:8] * 4.0 + (parts[8:16] - CENTRE)) * scale


def scale_rows(range_ref):
    index = lax.broadcasted_iota(jnp.int32, (8, 128), 0)
    picked = jnp.where(
        index == 0,
        range_ref[0],
        jnp.where(index == 1, range_ref[1], jnp.where(index == 2, range_ref[2], 0.0)),
    )
    return picked * LOG2E


def cov_kernel(halves, modes, core_ref, range_ref, row_ref, col_ref, *refs):
    count = len(halves)
    start_refs, refs = refs[: len(refs) - 2 - count], refs[len(refs) - 2 - count :]
    out_refs, (rows, cols) = refs[:count], refs[count:]
    pieces, _, width = col_ref.shape
    dests = row_ref.shape[0] // 2
    scale = scale_rows(range_ref)
    low = jnp.concatenate([col_ref[piece, 0:modes, :] for piece in range(pieces)], axis=1)
    for piece in range(pieces):
        coords = scaled_coords(col_ref[piece, modes : modes + 16, :], scale).T
        for d in range(3):
            cols[d, piece * width : (piece + 1) * width, :] = jnp.broadcast_to(coords[:, d : d + 1], (width, width))
    for which, half in enumerate(halves):
        core = core_ref[0] if half == 0 else 1 - core_ref[0]
        for y in range(dests):
            rows[which, :, y * width : (y + 1) * width] = scaled_coords(row_ref[2 * y + core], scale)
        for pair in range(dests // 2):
            parts = []
            for y in (2 * pair, 2 * pair + 1):
                total = LOG2E * LOG2E
                for d in range(3):
                    delta = cols[d] - rows[which, d : d + 1, y * width : (y + 1) * width]
                    total = total + delta * delta
                parts.append(jnp.exp2(LOG2E - total * lax.rsqrt(total)).astype(jnp.bfloat16))
            update = jnp.dot(low, jnp.concatenate(parts, axis=1), preferred_element_type=jnp.float32)
            for y in range(2):
                term = update[:, y * width : (y + 1) * width]
                if start_refs:
                    term = term + start_refs[which][2 * pair + y]
                out_refs[which][2 * pair + y] = term


def covariance_part(core, inv_range, row_pack, col_pack, halves, starts=()):
    dests, _, width = row_pack.shape
    dests = dests // 2
    modes = col_pack.shape[1] - 16
    pairs = col_pack.shape[0] * dests * width * width * len(halves)
    vmem = pl.BlockSpec(memory_space=pltpu.VMEM)
    smem = pl.BlockSpec(memory_space=pltpu.SMEM)
    args = (core, inv_range, row_pack, col_pack) + tuple(starts)
    return pl.pallas_call(
        functools.partial(cov_kernel, halves, modes),
        out_shape=[jax.ShapeDtypeStruct((dests, modes, width), jnp.float32)] * len(halves),
        in_specs=[smem, smem] + [vmem] * (len(args) - 2),
        out_specs=[vmem] * len(halves),
        scratch_shapes=[
            pltpu.VMEM((len(halves), 8, dests * width), jnp.float32),
            pltpu.VMEM((3, col_pack.shape[0] * width, width), jnp.float32),
        ],
        input_output_aliases={4 + k: k for k in range(len(starts))},
        compiler_params=PARAMS,
        cost_estimate=pl.CostEstimate(
            flops=pairs * 2 * modes * 4, bytes_accessed=4 * dests * modes * width, transcendentals=2 * pairs
        ),
    )(*args)


def nt_dot(left, right):
    return lax.dot_general(
        left, right, (((1,), (1,)), ((), ())), precision=HIGHEST, preferred_element_type=jnp.float32
    )


def prepare_kernel(coord_ref, mode_ref, block_ref, row_ref):
    coords = coord_ref[...].astype(jnp.float32)
    high = jnp.floor(coords * 0.25)
    blank = jnp.zeros((5, coords.shape[1]), jnp.float32)
    pack = jnp.concatenate([high, blank, coords - 4.0 * high, blank], axis=0).astype(jnp.bfloat16)
    for k in range(row_ref.shape[0]):
        row_ref[k] = pack
    pack = jnp.concatenate([mode_ref[...].astype(jnp.bfloat16), pack], axis=0)
    for k in range(block_ref.shape[0]):
        block_ref[k] = pack


def gram_kernel(part_ref, mode_ref, image_ref, gram_ref):
    image = part_ref[0]
    for y in range(1, part_ref.shape[0]):
        image = image + part_ref[y]
    mode = mode_ref[...]
    image = image + NUGGET * mode
    image_ref[...] = image
    modes, width = image.shape
    third = modes // 3
    blank = jnp.zeros((third, width), jnp.float32)
    one, two = mode[third : 2 * third], mode[2 * third :]
    left = jnp.concatenate(
        [image, jnp.concatenate([one, two, blank], axis=0), jnp.concatenate([blank, blank, two], axis=0)], axis=1
    )
    right = jnp.concatenate(
        [
            jnp.concatenate([image, jnp.zeros((modes, 2 * width), jnp.float32)], axis=1),
            jnp.concatenate([blank, one, two], axis=1),
        ],
        axis=0,
    )
    grams = (nt_dot(left, right), nt_dot(mode, jnp.concatenate([image, mode[:third]], axis=0)))
    tiles, slots = modes // 8, gram_ref.shape[0]
    for which, gram in enumerate(grams):
        for t in range(tiles):
            level, slot = divmod(which * tiles + t, slots)
            gram_ref[slot, level * 8 : level * 8 + 8, :] = gram[t * 8 : t * 8 + 8, :]


def spread_kernel(part_ref, out_ref):
    total = part_ref[0]
    for k in range(1, part_ref.shape[0]):
        total = total + part_ref[k]
    for k in range(out_ref.shape[0]):
        out_ref[k] = total


def final_kernel(node_total, gram_ref, image_ref, basis_ref, ritz_ref):
    modes, width = image_ref.shape
    tiles = modes // 8
    slots = gram_ref.shape[0]

    def tile(which, t):
        level, slot = divmod(which * tiles + t, slots)
        return gram_ref[slot, level * 8 : level * 8 + 8, :] * (1.0 / node_total)

    lane = lax.broadcasted_iota(jnp.int32, (8, width), 1)
    row = lax.broadcasted_iota(jnp.int32, (8, width), 0)
    third = modes // 3
    lower = []
    for t in range(tiles):
        block = 8 * t // third
        value = pltpu.roll(tile(1, t), third, 1)
        if block >= 1:
            moved = pltpu.roll(tile(0, t - third // 8), 2 * third, 1)
            value = jnp.where(lane < third, value, moved)
        if block == 2:
            moved = pltpu.roll(tile(0, t), 3 * third, 1)
            value = jnp.where(lane < 2 * third, value, moved)
        lower.append(jnp.where(lane < (block + 1) * third, value, 0.0))
    upper = jnp.concatenate(lower + [jnp.zeros((width - modes, width), jnp.float32)], axis=0).T
    left = [
        [tile(0, t) for t in range(tiles)],
        [
            jnp.where(lane < (8 * t // third + 1) * third, lower[t], upper[8 * t : 8 * t + 8, :])
            for t in range(tiles)
        ],
    ]
    right = [
        [image_ref[t * 8 : t * 8 + 8, :] for t in range(tiles)],
        [jnp.where(lane == row + 8 * t, 1.0, 0.0) for t in range(tiles)],
    ]
    for k in range(modes):
        home, sub = divmod(k, 8)
        for m in range(2):
            a, b = left[m], right[m]
            spread = {t: jnp.broadcast_to(a[t][:, k : k + 1], (8, width)) for t in range(home, tiles)}
            inverse = 1.0 / spread[home][sub : sub + 1, :]
            row_a = jnp.broadcast_to(a[home][sub : sub + 1, :] * inverse, (8, width))
            row_b = jnp.broadcast_to(b[home][sub : sub + 1, :] * inverse, (8, width))
            for t in range(home, tiles):
                factor = spread[t]
                if t == home:
                    if sub == 7:
                        continue
                    factor = jnp.where(row > sub, factor, 0.0)
                a[t] = a[t] - factor * row_a
                b[t] = b[t] - factor * row_b

    def finish(m):
        rows = []
        for t in range(tiles):
            pivot = jnp.sum(jnp.where(lane == row + 8 * t, left[m][t], 0.0), axis=1, keepdims=True)
            rows.append(right[m][t] * (1.0 / jnp.sqrt(pivot)))
        return jnp.concatenate(rows, axis=0)

    basis_ref[...] = finish(0)
    inverse = finish(1)[:, 0:modes]
    cross = jnp.concatenate([tile(1, t) for t in range(tiles)], axis=0)[:, 0:modes]
    half = jnp.dot(inverse, cross, precision=HIGHEST, preferred_element_type=jnp.float32)
    ritz_ref[...] = nt_dot(half, inverse)


def call(kernel, out_shape, *args):
    return pl.pallas_call(kernel, out_shape=out_shape, compiler_params=PARAMS)(*args)


def body(node_coords, inv_range, mode_block):
    modes, width = mode_block.shape
    across, depth, stripes, cores = (lax.axis_size(axis) for axis in ("x", "z", "y", "c"))
    node_total = across * depth * stripes * cores * width
    slots = stripes * cores
    block, row_pack = call(
        prepare_kernel,
        (
            jax.ShapeDtypeStruct((depth, modes + 16, width), jnp.bfloat16),
            jax.ShapeDtypeStruct((slots, 16, width), jnp.bfloat16),
        ),
        node_coords,
        mode_block,
    )
    block = lax.all_to_all(block, "z", 0, 0)
    beside = lax.ppermute(block, "x", [(i, i ^ 1) for i in range(across)])
    row_pack = lax.all_to_all(row_pack, ("y", "c"), 0, 0)
    pair = jnp.concatenate([block, beside], axis=0)
    other = lax.ppermute(pair, "x", [(i, across - 1 - i) for i in range(across)])
    core = lax.axis_index("c").astype(jnp.int32)[None]
    shared = functools.partial(covariance_part, core, inv_range, row_pack)
    far, near = shared(block, (1, 0))
    far, near = shared(beside, (1, 0), (far, near))
    (far,) = shared(other, (1,), (far,))
    far = lax.ppermute(far, "c", [(0, 1), (1, 0)])
    (near,) = shared(other, (0,), (near,))
    pieces = lax.all_to_all(near + far, "y", 0, 0)
    slots = across * cores
    levels = -(-2 * (modes // 8) // slots)
    image, grams = call(
        gram_kernel,
        (
            jax.ShapeDtypeStruct((modes, width), jnp.float32),
            jax.ShapeDtypeStruct((slots, 8 * levels, width), jnp.float32),
        ),
        pieces,
        mode_block,
    )
    for axes, copies in ((("x", "c"), stripes), ("y", depth), ("z", slots)):
        grams = lax.all_to_all(grams, axes, 0, 0)
        grams = call(spread_kernel, jax.ShapeDtypeStruct((copies, 8 * levels, width), jnp.float32), grams)
    grams = lax.all_to_all(grams, ("x", "c"), 0, 0)
    basis, ritz = call(
        functools.partial(final_kernel, node_total),
        (
            jax.ShapeDtypeStruct((modes, width), jnp.float32),
            jax.ShapeDtypeStruct((modes, modes), jnp.float32),
        ),
        grams,
        image,
    )
    return (basis, ritz)


def solution(mesh):
    parts = Mesh(mesh.devices.reshape(4, mesh.devices.shape[0] // 4, -1, 2), ("x", "z", "y", "c"))
    nodes = P(None, ("x", "z", "y", "c"))
    return jax.shard_map(
        body, mesh=parts, in_specs=(nodes, P(), nodes), out_specs=(nodes, P()), check_vma=False
    )
```

```python
import functools
import math

import jax
import jax.numpy as jnp
from jax import lax
from jax.experimental import pallas as pl
from jax.experimental.pallas import tpu as pltpu
from jax.sharding import Mesh, PartitionSpec as P

NUGGET = 0.25
LOG2E = math.log2(math.e)
CENTRE = 512.0
HIGHEST = lax.Precision.HIGHEST
PARAMS = pltpu.CompilerParams(vmem_limit_bytes=48 * 1024 * 1024)


def scaled_coords(pack, scale):
    parts = pack.astype(jnp.float32)
    return (parts[0:8] * 4.0 + (parts[8:16] - CENTRE)) * scale


def scale_rows(range_ref):
    index = lax.broadcasted_iota(jnp.int32, (8, 128), 0)
    picked = jnp.where(
        index == 0,
        range_ref[0],
        jnp.where(index == 1, range_ref[1], jnp.where(index == 2, range_ref[2], 0.0)),
    )
    return picked * LOG2E


def cov_kernel(halves, modes, core_ref, range_ref, row_ref, col_ref, *refs):
    count = len(halves)
    start_refs, refs = refs[: len(refs) - 2 - count], refs[len(refs) - 2 - count :]
    out_refs, (rows, cols) = refs[:count], refs[count:]
    pieces, _, width = col_ref.shape
    dests = row_ref.shape[0] // 2
    scale = scale_rows(range_ref)
    low = jnp.concatenate([col_ref[piece, 0:modes, :] for piece in range(pieces)], axis=1)
    for piece in range(pieces):
        coords = scaled_coords(col_ref[piece, modes : modes + 16, :], scale).T
        for d in range(3):
            cols[d, piece * width : (piece + 1) * width, :] = jnp.broadcast_to(coords[:, d : d + 1], (width, width))
    for which, half in enumerate(halves):
        core = core_ref[0] if half == 0 else 1 - core_ref[0]
        for y in range(dests):
            rows[which, :, y * width : (y + 1) * width] = scaled_coords(row_ref[2 * y + core], scale)
        for pair in range(dests // 2):
            parts = []
            for y in (2 * pair, 2 * pair + 1):
                total = LOG2E * LOG2E
                for d in range(3):
                    delta = cols[d] - rows[which, d : d + 1, y * width : (y + 1) * width]
                    total = total + delta * delta
                parts.append(jnp.exp2(LOG2E - total * lax.rsqrt(total)).astype(jnp.bfloat16))
            update = jnp.dot(low, jnp.concatenate(parts, axis=1), preferred_element_type=jnp.float32)
            for y in range(2):
                term = update[:, y * width : (y + 1) * width]
                if start_refs:
                    term = term + start_refs[which][2 * pair + y]
                out_refs[which][2 * pair + y] = term


def covariance_part(core, inv_range, row_pack, col_pack, halves, starts=()):
    dests, _, width = row_pack.shape
    dests = dests // 2
    modes = col_pack.shape[1] - 16
    pairs = col_pack.shape[0] * dests * width * width * len(halves)
    vmem = pl.BlockSpec(memory_space=pltpu.VMEM)
    smem = pl.BlockSpec(memory_space=pltpu.SMEM)
    args = (core, inv_range, row_pack, col_pack) + tuple(starts)
    return pl.pallas_call(
        functools.partial(cov_kernel, halves, modes),
        out_shape=[jax.ShapeDtypeStruct((dests, modes, width), jnp.float32)] * len(halves),
        in_specs=[smem, smem] + [vmem] * (len(args) - 2),
        out_specs=[vmem] * len(halves),
        scratch_shapes=[
            pltpu.VMEM((len(halves), 8, dests * width), jnp.float32),
            pltpu.VMEM((3, col_pack.shape[0] * width, width), jnp.float32),
        ],
        input_output_aliases={4 + k: k for k in range(len(starts))},
        compiler_params=PARAMS,
        cost_estimate=pl.CostEstimate(
            flops=pairs * 2 * modes * 4, bytes_accessed=4 * dests * modes * width, transcendentals=2 * pairs
        ),
    )(*args)


def nt_dot(left, right):
    return lax.dot_general(
        left, right, (((1,), (1,)), ((), ())), precision=HIGHEST, preferred_element_type=jnp.float32
    )


def pack_coords(coord_ref):
    coords = coord_ref[...].astype(jnp.float32)
    high = jnp.floor(coords * 0.25)
    blank = jnp.zeros((5, coords.shape[1]), jnp.float32)
    return jnp.concatenate([high, blank, coords - 4.0 * high, blank], axis=0).astype(jnp.bfloat16)


def row_kernel(coord_ref, out_ref):
    pack = pack_coords(coord_ref)
    for k in range(out_ref.shape[0]):
        out_ref[k] = pack


def block_kernel(coord_ref, mode_ref, out_ref):
    pack = jnp.concatenate([mode_ref[...].astype(jnp.bfloat16), pack_coords(coord_ref)], axis=0)
    for k in range(out_ref.shape[0]):
        out_ref[k] = pack


def gram_kernel(part_ref, mode_ref, image_ref, gram_ref):
    image = part_ref[0]
    for y in range(1, part_ref.shape[0]):
        image = image + part_ref[y]
    mode = mode_ref[...]
    image = image + NUGGET * mode
    image_ref[...] = image
    modes, width = image.shape
    third = modes // 3
    blank = jnp.zeros((third, width), jnp.float32)
    one, two = mode[third : 2 * third], mode[2 * third :]
    left = jnp.concatenate(
        [image, jnp.concatenate([one, two, blank], axis=0), jnp.concatenate([blank, blank, two], axis=0)], axis=1
    )
    right = jnp.concatenate(
        [
            jnp.concatenate([image, jnp.zeros((modes, 2 * width), jnp.float32)], axis=1),
            jnp.concatenate([blank, one, two], axis=1),
        ],
        axis=0,
    )
    grams = (nt_dot(left, right), nt_dot(mode, jnp.concatenate([image, mode[:third]], axis=0)))
    tiles, slots = modes // 8, gram_ref.shape[0]
    for slot in range(2 * tiles % slots, slots):
        gram_ref[slot, gram_ref.shape[1] - 8 :, :] = jnp.zeros((8, width), jnp.float32)
    for which, gram in enumerate(grams):
        for t in range(tiles):
            level, slot = divmod(which * tiles + t, slots)
            gram_ref[slot, level * 8 : level * 8 + 8, :] = gram[t * 8 : t * 8 + 8, :]


def spread_kernel(part_ref, out_ref):
    total = part_ref[0]
    for k in range(1, part_ref.shape[0]):
        total = total + part_ref[k]
    for k in range(out_ref.shape[0]):
        out_ref[k] = total


def final_kernel(node_total, gram_ref, image_ref, basis_ref, ritz_ref):
    modes, width = image_ref.shape
    tiles = modes // 8
    slots = gram_ref.shape[0]

    def tile(which, t):
        level, slot = divmod(which * tiles + t, slots)
        return gram_ref[slot, level * 8 : level * 8 + 8, :] * (1.0 / node_total)

    lane = lax.broadcasted_iota(jnp.int32, (8, width), 1)
    row = lax.broadcasted_iota(jnp.int32, (8, width), 0)
    third = modes // 3
    lower = []
    for t in range(tiles):
        block = 8 * t // third
        value = pltpu.roll(tile(1, t), third, 1)
        if block >= 1:
            moved = pltpu.roll(tile(0, t - third // 8), 2 * third, 1)
            value = jnp.where(lane < third, value, moved)
        if block == 2:
            moved = pltpu.roll(tile(0, t), 3 * third, 1)
            value = jnp.where(lane < 2 * third, value, moved)
        lower.append(jnp.where(lane < (block + 1) * third, value, 0.0))
    upper = jnp.concatenate(lower + [jnp.zeros((width - modes, width), jnp.float32)], axis=0).T
    left = [
        [tile(0, t) for t in range(tiles)],
        [
            jnp.where(lane < (8 * t // third + 1) * third, lower[t], upper[8 * t : 8 * t + 8, :])
            for t in range(tiles)
        ],
    ]
    right = [
        [image_ref[t * 8 : t * 8 + 8, :] for t in range(tiles)],
        [jnp.where(lane == row + 8 * t, 1.0, 0.0) for t in range(tiles)],
    ]
    for m in range(2):
        picked = [jnp.where(lane == row + 8 * t, left[m][t], 0.0) for t in range(tiles)]
        across = jnp.sum(functools.reduce(jnp.add, picked), axis=0, keepdims=True)
        across = 1.0 / jnp.sqrt(jnp.where(lane[0:1] < modes, across, 1.0))
        for t in range(tiles):
            down = 1.0 / jnp.sqrt(jnp.sum(picked[t], axis=1, keepdims=True))
            left[m][t] = left[m][t] * down * across
            right[m][t] = right[m][t] * down

    def spread_row(value, i):
        return jnp.broadcast_to(value[i : i + 1, :], (8, width))

    def spread_lane(value, k):
        return jnp.broadcast_to(value[:, k : k + 1], (8, width))

    done = [[None] * tiles, [None] * tiles]
    for k in range(0, modes, 2):
        home, sub = divmod(k, 8)
        near = [(spread_lane(left[m][home], k), spread_lane(left[m][home], k + 1)) for m in range(2)]
        steps = []
        for m in range(2):
            first, second = near[m]
            p, q, r = spread_row(first, sub), spread_row(first, sub + 1), spread_row(second, sub + 1)
            a0, a1 = spread_row(left[m][home], sub), spread_row(left[m][home], sub + 1)
            b0, b1 = spread_row(right[m][home], sub), spread_row(right[m][home], sub + 1)
            scale = 1.0 / (p * r - q * q)
            steps.append(
                ((r * a0 - q * a1) * scale, (p * a1 - q * a0) * scale, (r * b0 - q * b1) * scale, (p * b1 - q * b0) * scale)
            )
            flat = 1.0 / p
            ratio = q * flat
            rows = jnp.where(row == sub, b0 * jnp.sqrt(flat), (b1 - ratio * b0) / jnp.sqrt(r - ratio * q))
            done[m][home] = rows if sub == 0 else jnp.where(row >= sub, rows, done[m][home])
        for t in range(home, tiles):
            for m in range(2):
                a, b = left[m], right[m]
                if t > home:
                    f0, f1 = spread_lane(a[t], k), spread_lane(a[t], k + 1)
                elif sub < 6:
                    f0, f1 = (jnp.where(row > sub + 1, part, 0.0) for part in near[m])
                else:
                    continue
                a0, a1, b0, b1 = steps[m]
                a[t] = a[t] - (f0 * a0 + f1 * a1)
                b[t] = b[t] - (f0 * b0 + f1 * b1)

    basis_ref[...] = jnp.concatenate(done[0], axis=0)
    inverse = jnp.concatenate(done[1], axis=0)[:, 0:modes]
    cross = jnp.concatenate([tile(1, t) for t in range(tiles)], axis=0)[:, 0:modes]
    half = jnp.dot(inverse, cross, precision=HIGHEST, preferred_element_type=jnp.float32)
    ritz_ref[...] = nt_dot(half, inverse)


def call(kernel, out_shape, *args):
    return pl.pallas_call(kernel, out_shape=out_shape, compiler_params=PARAMS)(*args)


def body(node_coords, inv_range, mode_block):
    modes, width = mode_block.shape
    near_axes, far_axes, last = ("xl", "zl", "yl"), ("zh", "yh"), "xh"
    count = {axis: lax.axis_size(axis) for axis in near_axes + far_axes + (last, "c")}
    dests, sources = (math.prod(count[axis] for axis in axes) for axes in (near_axes, far_axes))
    node_total = math.prod(count.values()) * width
    row_pack = call(row_kernel, jax.ShapeDtypeStruct((2 * dests, 16, width), jnp.bfloat16), node_coords)
    row_pack = lax.all_to_all(row_pack, near_axes + ("c",), 0, 0)
    block = call(
        block_kernel, jax.ShapeDtypeStruct((sources, modes + 16, width), jnp.bfloat16), node_coords, mode_block
    )
    block, row_pack = lax.optimization_barrier((block, row_pack))
    block = lax.all_to_all(block, far_axes, 0, 0)
    other = lax.ppermute(block, last, [(0, 1), (1, 0)])
    core = lax.axis_index("c").astype(jnp.int32)[None]
    shared = functools.partial(covariance_part, core, inv_range, row_pack)
    far, near = shared(block, (1, 0))
    (far,) = shared(other, (1,), (far,))
    far = lax.ppermute(far, "c", [(0, 1), (1, 0)])
    (near,) = shared(other, (0,), (near,))
    pieces = lax.all_to_all(near + far, near_axes, 0, 0)
    split_axes = (last,) + near_axes + ("c",)
    slots = math.prod(count[axis] for axis in split_axes)
    levels = -(-2 * (modes // 8) // slots)
    image, grams = call(
        gram_kernel,
        (
            jax.ShapeDtypeStruct((modes, width), jnp.float32),
            jax.ShapeDtypeStruct((slots, 8 * levels, width), jnp.float32),
        ),
        pieces,
        mode_block,
    )
    for axes, copies in ((split_axes, sources), (far_axes, slots)):
        grams = lax.all_to_all(grams, axes, 0, 0)
        grams = call(spread_kernel, jax.ShapeDtypeStruct((copies, 8 * levels, width), jnp.float32), grams)
    grams = lax.all_to_all(grams, split_axes, 0, 0)
    basis, ritz = call(
        functools.partial(final_kernel, node_total),
        (
            jax.ShapeDtypeStruct((modes, width), jnp.float32),
            jax.ShapeDtypeStruct((modes, modes), jnp.float32),
        ),
        grams,
        image,
    )
    return (basis, ritz)


def solution(mesh):
    axes = ("xh", "xl", "zh", "zl", "yh", "yl", "c")
    parts = Mesh(mesh.devices.reshape(2, 2, 4, 2, 4, 2, 2), axes)
    nodes = P(None, axes)
    return jax.shard_map(
        body, mesh=parts, in_specs=(nodes, P(), nodes), out_specs=(nodes, P()), check_vma=False
    )
```

```python
import functools
import math

import jax
import jax.numpy as jnp
from jax import lax
from jax.experimental import pallas as pl
from jax.experimental.pallas import tpu as pltpu
from jax.sharding import Mesh, PartitionSpec as P

NUGGET = 0.25
LOG2E = math.log2(math.e)
CENTRE = 512.0
HIGHEST = lax.Precision.HIGHEST
PARAMS = pltpu.CompilerParams(vmem_limit_bytes=48 * 1024 * 1024)


def scaled_coords(pack, scale):
    parts = pack.astype(jnp.float32)
    return (parts[0:8] * 4.0 + (parts[8:16] - CENTRE)) * scale


def scale_rows(range_ref):
    index = lax.broadcasted_iota(jnp.int32, (8, 128), 0)
    picked = jnp.where(
        index == 0,
        range_ref[0],
        jnp.where(index == 1, range_ref[1], jnp.where(index == 2, range_ref[2], 0.0)),
    )
    return picked * LOG2E


def cov_kernel(halves, modes, core_ref, range_ref, row_ref, col_ref, *refs):
    count = len(halves)
    start_refs, refs = refs[: len(refs) - 2 - count], refs[len(refs) - 2 - count :]
    out_refs, (rows, cols) = refs[:count], refs[count:]
    pieces, _, width = col_ref.shape
    dests = row_ref.shape[0] // 2
    scale = scale_rows(range_ref)
    low = jnp.concatenate([col_ref[piece, 0:modes, :] for piece in range(pieces)], axis=1)
    for piece in range(pieces):
        coords = scaled_coords(col_ref[piece, modes : modes + 16, :], scale).T
        for d in range(3):
            cols[d, piece * width : (piece + 1) * width, :] = jnp.broadcast_to(coords[:, d : d + 1], (width, width))
    for which, half in enumerate(halves):
        core = core_ref[0] if half == 0 else 1 - core_ref[0]
        for y in range(dests):
            rows[which, :, y * width : (y + 1) * width] = scaled_coords(row_ref[2 * y + core], scale)
        for pair in range(dests // 2):
            parts = []
            for y in (2 * pair, 2 * pair + 1):
                total = LOG2E * LOG2E
                for d in range(3):
                    delta = cols[d] - rows[which, d : d + 1, y * width : (y + 1) * width]
                    total = total + delta * delta
                parts.append(jnp.exp2(LOG2E - total * lax.rsqrt(total)).astype(jnp.bfloat16))
            update = jnp.dot(low, jnp.concatenate(parts, axis=1), preferred_element_type=jnp.float32)
            for y in range(2):
                term = update[:, y * width : (y + 1) * width]
                if start_refs:
                    term = term + start_refs[which][2 * pair + y]
                out_refs[which][2 * pair + y] = term


def covariance_part(core, inv_range, row_pack, col_pack, halves, starts=()):
    dests, _, width = row_pack.shape
    dests = dests // 2
    modes = col_pack.shape[1] - 16
    pairs = col_pack.shape[0] * dests * width * width * len(halves)
    vmem = pl.BlockSpec(memory_space=pltpu.VMEM)
    smem = pl.BlockSpec(memory_space=pltpu.SMEM)
    args = (core, inv_range, row_pack, col_pack) + tuple(starts)
    return pl.pallas_call(
        functools.partial(cov_kernel, halves, modes),
        out_shape=[jax.ShapeDtypeStruct((dests, modes, width), jnp.float32)] * len(halves),
        in_specs=[smem, smem] + [vmem] * (len(args) - 2),
        out_specs=[vmem] * len(halves),
        scratch_shapes=[
            pltpu.VMEM((len(halves), 8, dests * width), jnp.float32),
            pltpu.VMEM((3, col_pack.shape[0] * width, width), jnp.float32),
        ],
        input_output_aliases={4 + k: k for k in range(len(starts))},
        compiler_params=PARAMS,
        cost_estimate=pl.CostEstimate(
            flops=pairs * 2 * modes * 4, bytes_accessed=4 * dests * modes * width, transcendentals=2 * pairs
        ),
    )(*args)


def nt_dot(left, right):
    return lax.dot_general(
        left, right, (((1,), (1,)), ((), ())), precision=HIGHEST, preferred_element_type=jnp.float32
    )


def pack_coords(coord_ref):
    coords = coord_ref[...].astype(jnp.float32)
    high = jnp.floor(coords * 0.25)
    blank = jnp.zeros((5, coords.shape[1]), jnp.float32)
    return jnp.concatenate([high, blank, coords - 4.0 * high, blank], axis=0).astype(jnp.bfloat16)


def row_kernel(coord_ref, out_ref):
    pack = pack_coords(coord_ref)
    for k in range(out_ref.shape[0]):
        out_ref[k] = pack


def block_kernel(coord_ref, mode_ref, out_ref):
    pack = jnp.concatenate([mode_ref[...].astype(jnp.bfloat16), pack_coords(coord_ref)], axis=0)
    for k in range(out_ref.shape[0]):
        out_ref[k] = pack


def gram_kernel(part_ref, mode_ref, image_ref, gram_ref):
    image = part_ref[0]
    for y in range(1, part_ref.shape[0]):
        image = image + part_ref[y]
    mode = mode_ref[...]
    image = image + NUGGET * mode
    image_ref[...] = image
    modes, width = image.shape
    third = modes // 3
    blank = jnp.zeros((third, width), jnp.float32)
    one, two = mode[third : 2 * third], mode[2 * third :]
    left = jnp.concatenate(
        [image, jnp.concatenate([one, two, blank], axis=0), jnp.concatenate([blank, blank, two], axis=0)], axis=1
    )
    right = jnp.concatenate(
        [
            jnp.concatenate([image, jnp.zeros((modes, 2 * width), jnp.float32)], axis=1),
            jnp.concatenate([blank, one, two], axis=1),
        ],
        axis=0,
    )
    grams = (nt_dot(left, right), nt_dot(mode, jnp.concatenate([image, mode[:third]], axis=0)))
    tiles, slots = modes // 8, gram_ref.shape[0]
    for slot in range(2 * tiles % slots, slots):
        gram_ref[slot, gram_ref.shape[1] - 8 :, :] = jnp.zeros((8, width), jnp.float32)
    for which, gram in enumerate(grams):
        for t in range(tiles):
            level, slot = divmod(which * tiles + t, slots)
            gram_ref[slot, level * 8 : level * 8 + 8, :] = gram[t * 8 : t * 8 + 8, :]


def spread_kernel(part_ref, out_ref):
    total = part_ref[0]
    for k in range(1, part_ref.shape[0]):
        total = total + part_ref[k]
    for k in range(out_ref.shape[0]):
        out_ref[k] = total


def final_kernel(node_total, gram_ref, image_ref, basis_ref, ritz_ref):
    modes, width = image_ref.shape
    tiles = modes // 8
    slots = gram_ref.shape[0]

    def tile(which, t):
        level, slot = divmod(which * tiles + t, slots)
        return gram_ref[slot, level * 8 : level * 8 + 8, :] * (1.0 / node_total)

    lane = lax.broadcasted_iota(jnp.int32, (8, width), 1)
    row = lax.broadcasted_iota(jnp.int32, (8, width), 0)
    third = modes // 3
    lower = []
    for t in range(tiles):
        block = 8 * t // third
        value = pltpu.roll(tile(1, t), third, 1)
        if block >= 1:
            moved = pltpu.roll(tile(0, t - third // 8), 2 * third, 1)
            value = jnp.where(lane < third, value, moved)
        if block == 2:
            moved = pltpu.roll(tile(0, t), 3 * third, 1)
            value = jnp.where(lane < 2 * third, value, moved)
        lower.append(jnp.where(lane < (block + 1) * third, value, 0.0))
    upper = jnp.concatenate(lower + [jnp.zeros((width - modes, width), jnp.float32)], axis=0).T
    left = [
        [tile(0, t) for t in range(tiles)],
        [
            jnp.where(lane < (8 * t // third + 1) * third, lower[t], upper[8 * t : 8 * t + 8, :])
            for t in range(tiles)
        ],
    ]
    right = [
        [image_ref[t * 8 : t * 8 + 8, :] for t in range(tiles)],
        [jnp.where(lane == row + 8 * t, 1.0, 0.0) for t in range(tiles)],
    ]
    for m in range(2):
        picked = [jnp.where(lane == row + 8 * t, left[m][t], 0.0) for t in range(tiles)]
        across = jnp.sum(functools.reduce(jnp.add, picked), axis=0, keepdims=True)
        across = 1.0 / jnp.sqrt(jnp.where(lane[0:1] < modes, across, 1.0))
        for t in range(tiles):
            down = 1.0 / jnp.sqrt(jnp.sum(picked[t], axis=1, keepdims=True))
            left[m][t] = left[m][t] * down * across
            right[m][t] = right[m][t] * down

    def spread_row(value, i):
        return jnp.broadcast_to(value[i : i + 1, :], (8, width))

    def spread_lane(value, k):
        return jnp.broadcast_to(value[:, k : k + 1], (8, width))

    done = [[None] * tiles, [None] * tiles]
    for k in range(0, modes, 2):
        home, sub = divmod(k, 8)
        near = [(spread_lane(left[m][home], k), spread_lane(left[m][home], k + 1)) for m in range(2)]
        steps = []
        for m in range(2):
            first, second = near[m]
            p, q, r = spread_row(first, sub), spread_row(first, sub + 1), spread_row(second, sub + 1)
            a0, a1 = spread_row(left[m][home], sub), spread_row(left[m][home], sub + 1)
            b0, b1 = spread_row(right[m][home], sub), spread_row(right[m][home], sub + 1)
            scale = 1.0 / (p * r - q * q)
            steps.append(
                ((r * a0 - q * a1) * scale, (p * a1 - q * a0) * scale, (r * b0 - q * b1) * scale, (p * b1 - q * b0) * scale)
            )
            flat = 1.0 / p
            ratio = q * flat
            rows = jnp.where(row == sub, b0 * jnp.sqrt(flat), (b1 - ratio * b0) / jnp.sqrt(r - ratio * q))
            done[m][home] = rows if sub == 0 else jnp.where(row >= sub, rows, done[m][home])
        for t in range(home, tiles):
            for m in range(2):
                a, b = left[m], right[m]
                if t > home:
                    f0, f1 = spread_lane(a[t], k), spread_lane(a[t], k + 1)
                elif sub < 6:
                    f0, f1 = (jnp.where(row > sub + 1, part, 0.0) for part in near[m])
                else:
                    continue
                a0, a1, b0, b1 = steps[m]
                a[t] = a[t] - (f0 * a0 + f1 * a1)
                b[t] = b[t] - (f0 * b0 + f1 * b1)

    basis_ref[...] = jnp.concatenate(done[0], axis=0)
    inverse = jnp.concatenate(done[1], axis=0)[:, 0:modes]
    cross = jnp.concatenate([tile(1, t) for t in range(tiles)], axis=0)[:, 0:modes]
    half = jnp.dot(inverse, cross, precision=HIGHEST, preferred_element_type=jnp.float32)
    ritz_ref[...] = nt_dot(half, inverse)


def call(kernel, out_shape, *args):
    return pl.pallas_call(kernel, out_shape=out_shape, compiler_params=PARAMS)(*args)


def body(node_coords, inv_range, mode_block):
    modes, width = mode_block.shape
    near_axes, far_axes, ring = ("xh", "xl", "yl"), ("zh", "zl"), "yh"
    split_axes, joint_axes = ("xh", "xl", "zl", "yl", "c"), ("zh", "yh")
    count = {axis: lax.axis_size(axis) for axis in near_axes + far_axes + (ring, "c")}
    dests, sources = (math.prod(count[axis] for axis in axes) for axes in (near_axes, far_axes))
    node_total = math.prod(count.values()) * width
    row_pack = call(row_kernel, jax.ShapeDtypeStruct((2 * dests, 16, width), jnp.bfloat16), node_coords)
    row_pack = lax.all_to_all(row_pack, near_axes + ("c",), 0, 0)
    block = call(
        block_kernel, jax.ShapeDtypeStruct((sources, modes + 16, width), jnp.bfloat16), node_coords, mode_block
    )
    block, row_pack = lax.optimization_barrier((block, row_pack))
    block = lax.all_to_all(block, far_axes, 0, 0)
    around = count[ring]
    order = [1, around - 1] + list(range(2, around - 1))
    others = [lax.ppermute(block, ring, [(i, (i + shift) % around) for i in range(around)]) for shift in order]
    core = lax.axis_index("c").astype(jnp.int32)[None]
    shared = functools.partial(covariance_part, core, inv_range, row_pack)
    far, near = shared(block, (1, 0))
    for other in others[:-1]:
        far, near = shared(other, (1, 0), (far, near))
    (far,) = shared(others[-1], (1,), (far,))
    far = lax.ppermute(far, "c", [(0, 1), (1, 0)])
    (near,) = shared(others[-1], (0,), (near,))
    pieces = lax.all_to_all(near + far, near_axes, 0, 0)
    slots, joined = (math.prod(count[axis] for axis in axes) for axes in (split_axes, joint_axes))
    levels = -(-2 * (modes // 8) // slots)
    image, grams = call(
        gram_kernel,
        (
            jax.ShapeDtypeStruct((modes, width), jnp.float32),
            jax.ShapeDtypeStruct((slots, 8 * levels, width), jnp.float32),
        ),
        pieces,
        mode_block,
    )
    for axes, copies in ((split_axes, joined), (joint_axes, slots)):
        grams = lax.all_to_all(grams, axes, 0, 0)
        grams = call(spread_kernel, jax.ShapeDtypeStruct((copies, 8 * levels, width), jnp.float32), grams)
    grams = lax.all_to_all(grams, split_axes, 0, 0)
    basis, ritz = call(
        functools.partial(final_kernel, node_total),
        (
            jax.ShapeDtypeStruct((modes, width), jnp.float32),
            jax.ShapeDtypeStruct((modes, modes), jnp.float32),
        ),
        grams,
        image,
    )
    return (basis, ritz)


def solution(mesh):
    axes = ("xh", "xl", "zh", "zl", "yh", "yl", "c")
    parts = Mesh(mesh.devices.reshape(2, 2, 4, 2, 4, 2, 2), axes)
    nodes = P(None, axes)
    return jax.shard_map(
        body, mesh=parts, in_specs=(nodes, P(), nodes), out_specs=(nodes, P()), check_vma=False
    )
```

```python
import functools
import math

import jax
import jax.numpy as jnp
from jax import lax
from jax.experimental import pallas as pl
from jax.experimental.pallas import tpu as pltpu
from jax.sharding import Mesh, PartitionSpec as P

NUGGET = 0.25
LOG2E = math.log2(math.e)
HIGHEST = lax.Precision.HIGHEST
PARAMS = pltpu.CompilerParams(vmem_limit_bytes=48 * 1024 * 1024)


def scale_rows(range_ref):
    index = lax.broadcasted_iota(jnp.int32, (8, 128), 0)
    picked = jnp.where(
        index == 0,
        range_ref[0],
        jnp.where(index == 1, range_ref[1], jnp.where(index == 2, range_ref[2], 0.0)),
    )
    return picked * LOG2E


def split(pack, centre):
    parts = pack.astype(jnp.float32)
    return (parts[0:8] - centre) * 4.0, parts[8:16]


def three_parts(value):
    one = value.astype(jnp.bfloat16).astype(jnp.float32)
    two = (value - one).astype(jnp.bfloat16).astype(jnp.float32)
    return [one, two, value - one - two]


def cov_kernel(halves, modes, core_ref, range_ref, row_ref, col_ref, *refs):
    count = len(halves)
    start_refs, refs = refs[: len(refs) - 2 - count], refs[len(refs) - 2 - count :]
    out_refs, (rows, cols) = refs[:count], refs[count:]
    pieces, _, width = col_ref.shape
    dests = row_ref.shape[0] // 2
    weight = scale_rows(range_ref)
    weight = weight * weight
    ones, blank = jnp.ones((1, width), jnp.float32), jnp.zeros((8, width), jnp.float32)
    total = sum(row_ref[k, 0:8, :].astype(jnp.float32) for k in range(2 * dests))
    centre = jnp.round(jnp.sum(total, axis=1, keepdims=True) * (1.0 / (2 * dests * width)))
    low = jnp.concatenate([col_ref[piece, 0:modes, :] for piece in range(pieces)], axis=1)
    for piece in range(pieces):
        high, rest = split(col_ref[piece, modes : modes + 16, :], centre)
        norm = jnp.sum(weight * (high + rest) * (high + rest), axis=0, keepdims=True)
        norms = jnp.concatenate([ones] * 3 + three_parts(norm) + [blank[0:2]], axis=0)
        features = jnp.concatenate([high] * 3 + [rest] * 3 + [norms, blank], axis=0)
        cols[piece * width : (piece + 1) * width, :] = features.T.astype(jnp.bfloat16)
    for which, half in enumerate(halves):
        core = core_ref[0] if half == 0 else 1 - core_ref[0]
        for y in range(dests):
            high, rest = split(row_ref[2 * y + core], centre)
            place = high + rest
            norm = jnp.sum(weight * place * place, axis=0, keepdims=True) + LOG2E * LOG2E
            norms = jnp.concatenate(three_parts(norm) + [ones] * 3 + [blank[0:2]], axis=0)
            cross = three_parts(-2.0 * weight * place)
            features = jnp.concatenate(cross + cross + [norms, blank], axis=0)
            rows[which, :, y * width : (y + 1) * width] = features.astype(jnp.bfloat16)
        group = 4
        for first in range(0, dests, group):
            span = slice(first * width, (first + group) * width)
            total = jnp.dot(cols[...], rows[which, :, span], preferred_element_type=jnp.float32)
            total = jnp.maximum(total, LOG2E * LOG2E)
            cov = jnp.exp2(LOG2E - total * lax.rsqrt(total)).astype(jnp.bfloat16)
            update = jnp.dot(low, cov, preferred_element_type=jnp.float32)
            for y in range(group):
                term = update[:, y * width : (y + 1) * width]
                if start_refs:
                    term = term + start_refs[which][first + y]
                out_refs[which][first + y] = term


def covariance_part(core, inv_range, row_pack, col_pack, halves, starts=()):
    dests, _, width = row_pack.shape
    dests = dests // 2
    modes = col_pack.shape[1] - 16
    pairs = col_pack.shape[0] * dests * width * width * len(halves)
    vmem = pl.BlockSpec(memory_space=pltpu.VMEM)
    smem = pl.BlockSpec(memory_space=pltpu.SMEM)
    args = (core, inv_range, row_pack, col_pack) + tuple(starts)
    return pl.pallas_call(
        functools.partial(cov_kernel, halves, modes),
        out_shape=[jax.ShapeDtypeStruct((dests, modes, width), jnp.float32)] * len(halves),
        in_specs=[smem, smem] + [vmem] * (len(args) - 2),
        out_specs=[vmem] * len(halves),
        scratch_shapes=[
            pltpu.VMEM((len(halves), 64, dests * width), jnp.bfloat16),
            pltpu.VMEM((col_pack.shape[0] * width, 64), jnp.bfloat16),
        ],
        input_output_aliases={4 + k: k for k in range(len(starts))},
        compiler_params=PARAMS,
        cost_estimate=pl.CostEstimate(
            flops=pairs * 2 * modes * 4, bytes_accessed=4 * dests * modes * width, transcendentals=2 * pairs
        ),
    )(*args)


def nt_dot(left, right):
    return lax.dot_general(
        left, right, (((1,), (1,)), ((), ())), precision=HIGHEST, preferred_element_type=jnp.float32
    )


def pack_coords(coord_ref):
    coords = coord_ref[...].astype(jnp.float32)
    high = jnp.floor(coords * 0.25)
    blank = jnp.zeros((5, coords.shape[1]), jnp.float32)
    return jnp.concatenate([high, blank, coords - 4.0 * high, blank], axis=0).astype(jnp.bfloat16)


def row_kernel(coord_ref, out_ref):
    pack = pack_coords(coord_ref)
    for k in range(out_ref.shape[0]):
        out_ref[k] = pack


def block_kernel(coord_ref, mode_ref, out_ref):
    pack = jnp.concatenate([mode_ref[...].astype(jnp.bfloat16), pack_coords(coord_ref)], axis=0)
    for k in range(out_ref.shape[0]):
        out_ref[k] = pack


def gram_kernel(part_ref, mode_ref, image_ref, gram_ref):
    image = part_ref[0]
    for y in range(1, part_ref.shape[0]):
        image = image + part_ref[y]
    mode = mode_ref[...]
    image = image + NUGGET * mode
    image_ref[...] = image
    modes, width = image.shape
    third = modes // 3
    blank = jnp.zeros((third, width), jnp.float32)
    one, two = mode[third : 2 * third], mode[2 * third :]
    left = jnp.concatenate(
        [image, jnp.concatenate([one, two, blank], axis=0), jnp.concatenate([blank, blank, two], axis=0)], axis=1
    )
    right = jnp.concatenate(
        [
            jnp.concatenate([image, jnp.zeros((modes, 2 * width), jnp.float32)], axis=1),
            jnp.concatenate([blank, one, two], axis=1),
        ],
        axis=0,
    )
    grams = (nt_dot(left, right), nt_dot(mode, jnp.concatenate([image, mode[:third]], axis=0)))
    tiles, slots = modes // 8, gram_ref.shape[0]
    for slot in range(2 * tiles % slots, slots):
        gram_ref[slot, gram_ref.shape[1] - 8 :, :] = jnp.zeros((8, width), jnp.float32)
    for which, gram in enumerate(grams):
        for t in range(tiles):
            level, slot = divmod(which * tiles + t, slots)
            gram_ref[slot, level * 8 : level * 8 + 8, :] = gram[t * 8 : t * 8 + 8, :]


def spread_kernel(part_ref, out_ref):
    total = part_ref[0]
    for k in range(1, part_ref.shape[0]):
        total = total + part_ref[k]
    for k in range(out_ref.shape[0]):
        out_ref[k] = total


def final_kernel(node_total, gram_ref, image_ref, basis_ref, ritz_ref):
    modes, width = image_ref.shape
    tiles = modes // 8
    slots = gram_ref.shape[0]

    def tile(which, t):
        level, slot = divmod(which * tiles + t, slots)
        return gram_ref[slot, level * 8 : level * 8 + 8, :] * (1.0 / node_total)

    lane = lax.broadcasted_iota(jnp.int32, (8, width), 1)
    row = lax.broadcasted_iota(jnp.int32, (8, width), 0)
    third = modes // 3
    lower = []
    for t in range(tiles):
        block = 8 * t // third
        value = pltpu.roll(tile(1, t), third, 1)
        if block >= 1:
            moved = pltpu.roll(tile(0, t - third // 8), 2 * third, 1)
            value = jnp.where(lane < third, value, moved)
        if block == 2:
            moved = pltpu.roll(tile(0, t), 3 * third, 1)
            value = jnp.where(lane < 2 * third, value, moved)
        lower.append(jnp.where(lane < (block + 1) * third, value, 0.0))
    upper = jnp.concatenate(lower + [jnp.zeros((width - modes, width), jnp.float32)], axis=0).T
    left = [
        [tile(0, t) for t in range(tiles)],
        [
            jnp.where(lane < (8 * t // third + 1) * third, lower[t], upper[8 * t : 8 * t + 8, :])
            for t in range(tiles)
        ],
    ]
    right = [
        [image_ref[t * 8 : t * 8 + 8, :] for t in range(tiles)],
        [jnp.where(lane == row + 8 * t, 1.0, 0.0) for t in range(tiles)],
    ]
    for m in range(2):
        picked = [jnp.where(lane == row + 8 * t, left[m][t], 0.0) for t in range(tiles)]
        across = jnp.sum(functools.reduce(jnp.add, picked), axis=0, keepdims=True)
        across = 1.0 / jnp.sqrt(jnp.where(lane[0:1] < modes, across, 1.0))
        for t in range(tiles):
            down = 1.0 / jnp.sqrt(jnp.sum(picked[t], axis=1, keepdims=True))
            left[m][t] = left[m][t] * down * across
            right[m][t] = right[m][t] * down

    def spread_row(value, i):
        return jnp.broadcast_to(value[i : i + 1, :], (8, width))

    def spread_lane(value, k):
        return jnp.broadcast_to(value[:, k : k + 1], (8, width))

    done = [[None] * tiles, [None] * tiles]
    for k in range(0, modes, 2):
        home, sub = divmod(k, 8)
        near = [(spread_lane(left[m][home], k), spread_lane(left[m][home], k + 1)) for m in range(2)]
        steps = []
        for m in range(2):
            first, second = near[m]
            p, q, r = spread_row(first, sub), spread_row(first, sub + 1), spread_row(second, sub + 1)
            a0, a1 = spread_row(left[m][home], sub), spread_row(left[m][home], sub + 1)
            b0, b1 = spread_row(right[m][home], sub), spread_row(right[m][home], sub + 1)
            scale = 1.0 / (p * r - q * q)
            steps.append(
                ((r * a0 - q * a1) * scale, (p * a1 - q * a0) * scale, (r * b0 - q * b1) * scale, (p * b1 - q * b0) * scale)
            )
            flat = 1.0 / p
            ratio = q * flat
            rows = jnp.where(row == sub, b0 * jnp.sqrt(flat), (b1 - ratio * b0) / jnp.sqrt(r - ratio * q))
            done[m][home] = rows if sub == 0 else jnp.where(row >= sub, rows, done[m][home])
        for t in range(home, tiles):
            for m in range(2):
                a, b = left[m], right[m]
                if t > home:
                    f0, f1 = spread_lane(a[t], k), spread_lane(a[t], k + 1)
                elif sub < 6:
                    f0, f1 = (jnp.where(row > sub + 1, part, 0.0) for part in near[m])
                else:
                    continue
                a0, a1, b0, b1 = steps[m]
                a[t] = a[t] - (f0 * a0 + f1 * a1)
                b[t] = b[t] - (f0 * b0 + f1 * b1)

    basis_ref[...] = jnp.concatenate(done[0], axis=0)
    inverse = jnp.concatenate(done[1], axis=0)[:, 0:modes]
    cross = jnp.concatenate([tile(1, t) for t in range(tiles)], axis=0)[:, 0:modes]
    half = jnp.dot(inverse, cross, precision=HIGHEST, preferred_element_type=jnp.float32)
    ritz_ref[...] = nt_dot(half, inverse)


def call(kernel, out_shape, *args):
    return pl.pallas_call(kernel, out_shape=out_shape, compiler_params=PARAMS)(*args)


def body(node_coords, inv_range, mode_block):
    modes, width = mode_block.shape
    near_axes, far_axes, last = ("xl", "zl", "yl"), ("zh", "yh"), "xh"
    count = {axis: lax.axis_size(axis) for axis in near_axes + far_axes + (last, "c")}
    dests, sources = (math.prod(count[axis] for axis in axes) for axes in (near_axes, far_axes))
    node_total = math.prod(count.values()) * width
    row_pack = call(row_kernel, jax.ShapeDtypeStruct((2 * dests, 16, width), jnp.bfloat16), node_coords)
    row_pack = lax.all_to_all(row_pack, near_axes + ("c",), 0, 0)
    block = call(
        block_kernel, jax.ShapeDtypeStruct((sources, modes + 16, width), jnp.bfloat16), node_coords, mode_block
    )
    block, row_pack = lax.optimization_barrier((block, row_pack))
    block = lax.all_to_all(block, far_axes, 0, 0)
    other = lax.ppermute(block, last, [(0, 1), (1, 0)])
    core = lax.axis_index("c").astype(jnp.int32)[None]
    shared = functools.partial(covariance_part, core, inv_range, row_pack)
    far, near = shared(block, (1, 0))
    (far,) = shared(other, (1,), (far,))
    far = lax.ppermute(far, "c", [(0, 1), (1, 0)])
    (near,) = shared(other, (0,), (near,))
    pieces = lax.all_to_all(near + far, near_axes, 0, 0)
    split_axes = (last,) + near_axes + ("c",)
    slots = math.prod(count[axis] for axis in split_axes)
    levels = -(-2 * (modes // 8) // slots)
    image, grams = call(
        gram_kernel,
        (
            jax.ShapeDtypeStruct((modes, width), jnp.float32),
            jax.ShapeDtypeStruct((slots, 8 * levels, width), jnp.float32),
        ),
        pieces,
        mode_block,
    )
    for axes, copies in ((split_axes, sources), (far_axes, slots)):
        grams = lax.all_to_all(grams, axes, 0, 0)
        grams = call(spread_kernel, jax.ShapeDtypeStruct((copies, 8 * levels, width), jnp.float32), grams)
    grams = lax.all_to_all(grams, split_axes, 0, 0)
    basis, ritz = call(
        functools.partial(final_kernel, node_total),
        (
            jax.ShapeDtypeStruct((modes, width), jnp.float32),
            jax.ShapeDtypeStruct((modes, modes), jnp.float32),
        ),
        grams,
        image,
    )
    return (basis, ritz)


def solution(mesh):
    axes = ("xh", "xl", "zh", "zl", "yh", "yl", "c")
    parts = Mesh(mesh.devices.reshape(2, 2, 4, 2, 4, 2, 2), axes)
    nodes = P(None, axes)
    return jax.shard_map(
        body, mesh=parts, in_specs=(nodes, P(), nodes), out_specs=(nodes, P()), check_vma=False
    )
```

```python
import functools
import math

import jax
import jax.numpy as jnp
from jax import lax
from jax.experimental import pallas as pl
from jax.experimental.pallas import tpu as pltpu
from jax.sharding import Mesh, PartitionSpec as P

NUGGET = 0.25
LOG2E = math.log2(math.e)
HIGHEST = lax.Precision.HIGHEST
PARAMS = pltpu.CompilerParams(vmem_limit_bytes=48 * 1024 * 1024)


def scale_rows(range_ref):
    index = lax.broadcasted_iota(jnp.int32, (8, 128), 0)
    picked = jnp.where(
        index == 0,
        range_ref[0],
        jnp.where(index == 1, range_ref[1], jnp.where(index == 2, range_ref[2], 0.0)),
    )
    return picked * LOG2E


def split(pack, centre):
    parts = pack.astype(jnp.float32)
    return (parts[0:8] - centre) * 4.0, parts[8:16]


def three_parts(value):
    one = value.astype(jnp.bfloat16).astype(jnp.float32)
    two = (value - one).astype(jnp.bfloat16).astype(jnp.float32)
    return [one, two, value - one - two]


def cov_kernel(halves, modes, core_ref, weight_ref, row_ref, col_ref, *refs):
    count = len(halves)
    start_refs, refs = refs[: len(refs) - 2 - count], refs[len(refs) - 2 - count :]
    out_refs, (rows, cols) = refs[:count], refs[count:]
    pieces, _, width = col_ref.shape
    dests = row_ref.shape[0] // 2
    weight = weight_ref[...]
    ones, blank = jnp.ones((1, width), jnp.float32), jnp.zeros((8, width), jnp.float32)
    total = sum(row_ref[k, 0:8, :].astype(jnp.float32) for k in range(2 * dests))
    centre = jnp.round(jnp.sum(total, axis=1, keepdims=True) * (1.0 / (2 * dests * width)))
    low = jnp.concatenate([col_ref[piece, 0:modes, :] for piece in range(pieces)], axis=1)
    for piece in range(pieces):
        high, rest = split(col_ref[piece, modes : modes + 16, :], centre)
        norm = jnp.sum(weight * (high + rest) * (high + rest), axis=0, keepdims=True)
        norms = jnp.concatenate([ones] * 3 + three_parts(norm) + [blank[0:2]], axis=0)
        features = jnp.concatenate([high] * 3 + [rest] * 3 + [norms, blank], axis=0)
        cols[piece * width : (piece + 1) * width, :] = features.T.astype(jnp.bfloat16)
    for which, half in enumerate(halves):
        core = core_ref[0] if half == 0 else 1 - core_ref[0]
        for y in range(dests):
            high, rest = split(row_ref[2 * y + core], centre)
            place = high + rest
            norm = jnp.sum(weight * place * place, axis=0, keepdims=True) + LOG2E * LOG2E
            norms = jnp.concatenate(three_parts(norm) + [ones] * 3 + [blank[0:2]], axis=0)
            cross = three_parts(-2.0 * weight * place)
            features = jnp.concatenate(cross + cross + [norms, blank], axis=0)
            rows[which, :, y * width : (y + 1) * width] = features.astype(jnp.bfloat16)
        group = 4
        for first in range(0, dests, group):
            span = slice(first * width, (first + group) * width)
            total = jnp.dot(cols[...], rows[which, :, span], preferred_element_type=jnp.float32)
            total = jnp.maximum(total, LOG2E * LOG2E)
            cov = jnp.exp2(LOG2E - total * lax.rsqrt(total)).astype(jnp.bfloat16)
            update = jnp.dot(low, cov, preferred_element_type=jnp.float32)
            for y in range(group):
                term = update[:, y * width : (y + 1) * width]
                if start_refs:
                    term = term + start_refs[which][first + y]
                out_refs[which][first + y] = term


def covariance_part(core, weight, row_pack, col_pack, halves, starts=()):
    dests, _, width = row_pack.shape
    dests = dests // 2
    modes = col_pack.shape[1] - 16
    pairs = col_pack.shape[0] * dests * width * width * len(halves)
    vmem = pl.BlockSpec(memory_space=pltpu.VMEM)
    smem = pl.BlockSpec(memory_space=pltpu.SMEM)
    args = (core, weight, row_pack, col_pack) + tuple(starts)
    return pl.pallas_call(
        functools.partial(cov_kernel, halves, modes),
        out_shape=[jax.ShapeDtypeStruct((dests, modes, width), jnp.float32)] * len(halves),
        in_specs=[smem] + [vmem] * (len(args) - 1),
        out_specs=[vmem] * len(halves),
        scratch_shapes=[
            pltpu.VMEM((len(halves), 64, dests * width), jnp.bfloat16),
            pltpu.VMEM((col_pack.shape[0] * width, 64), jnp.bfloat16),
        ],
        input_output_aliases={4 + k: k for k in range(len(starts))},
        compiler_params=PARAMS,
        cost_estimate=pl.CostEstimate(
            flops=pairs * 2 * modes * 4, bytes_accessed=4 * dests * modes * width, transcendentals=2 * pairs
        ),
    )(*args)


def nt_dot(left, right):
    return lax.dot_general(
        left, right, (((1,), (1,)), ((), ())), precision=HIGHEST, preferred_element_type=jnp.float32
    )


def row_kernel(coord_ref, out_ref):
    coords = coord_ref[...].astype(jnp.float32)
    high = jnp.floor(coords * 0.25)
    blank = jnp.zeros((5, coords.shape[1]), jnp.float32)
    pack = jnp.concatenate([high, blank, coords - 4.0 * high, blank], axis=0).astype(jnp.bfloat16)
    for k in range(out_ref.shape[0]):
        out_ref[k] = pack


def block_kernel(range_ref, row_ref, mode_ref, out_ref, weight_ref):
    scale = scale_rows(range_ref)
    weight_ref[...] = scale * scale
    pack = jnp.concatenate([mode_ref[...].astype(jnp.bfloat16), row_ref[0]], axis=0)
    for k in range(out_ref.shape[0]):
        out_ref[k] = pack


def gram_kernel(part_ref, mode_ref, image_ref, gram_ref):
    image = part_ref[0]
    for y in range(1, part_ref.shape[0]):
        image = image + part_ref[y]
    mode = mode_ref[...]
    image = image + NUGGET * mode
    image_ref[...] = image
    modes, width = image.shape
    third = modes // 3
    blank = jnp.zeros((third, width), jnp.float32)
    one, two = mode[third : 2 * third], mode[2 * third :]
    left = jnp.concatenate(
        [image, jnp.concatenate([one, two, blank], axis=0), jnp.concatenate([blank, blank, two], axis=0)], axis=1
    )
    right = jnp.concatenate(
        [
            jnp.concatenate([image, jnp.zeros((modes, 2 * width), jnp.float32)], axis=1),
            jnp.concatenate([blank, one, two], axis=1),
        ],
        axis=0,
    )
    grams = (nt_dot(left, right), nt_dot(mode, jnp.concatenate([image, mode[:third]], axis=0)))
    tiles, slots = modes // 8, gram_ref.shape[0]
    for slot in range(2 * tiles % slots, slots):
        gram_ref[slot, gram_ref.shape[1] - 8 :, :] = jnp.zeros((8, width), jnp.float32)
    for which, gram in enumerate(grams):
        for t in range(tiles):
            level, slot = divmod(which * tiles + t, slots)
            gram_ref[slot, level * 8 : level * 8 + 8, :] = gram[t * 8 : t * 8 + 8, :]


def spread_kernel(part_ref, out_ref):
    total = part_ref[0]
    for k in range(1, part_ref.shape[0]):
        total = total + part_ref[k]
    for k in range(out_ref.shape[0]):
        out_ref[k] = total


def final_kernel(node_total, gram_ref, image_ref, basis_ref, ritz_ref):
    modes, width = image_ref.shape
    tiles = modes // 8
    slots = gram_ref.shape[0]

    def tile(which, t):
        level, slot = divmod(which * tiles + t, slots)
        return gram_ref[slot, level * 8 : level * 8 + 8, :] * (1.0 / node_total)

    lane = lax.broadcasted_iota(jnp.int32, (8, width), 1)
    row = lax.broadcasted_iota(jnp.int32, (8, width), 0)
    third = modes // 3
    lower = []
    for t in range(tiles):
        block = 8 * t // third
        value = pltpu.roll(tile(1, t), third, 1)
        if block >= 1:
            moved = pltpu.roll(tile(0, t - third // 8), 2 * third, 1)
            value = jnp.where(lane < third, value, moved)
        if block == 2:
            moved = pltpu.roll(tile(0, t), 3 * third, 1)
            value = jnp.where(lane < 2 * third, value, moved)
        lower.append(jnp.where(lane < (block + 1) * third, value, 0.0))
    upper = jnp.concatenate(lower + [jnp.zeros((width - modes, width), jnp.float32)], axis=0).T
    left = [
        [tile(0, t) for t in range(tiles)],
        [
            jnp.where(lane < (8 * t // third + 1) * third, lower[t], upper[8 * t : 8 * t + 8, :])
            for t in range(tiles)
        ],
    ]
    right = [
        [image_ref[t * 8 : t * 8 + 8, :] for t in range(tiles)],
        [jnp.where(lane == row + 8 * t, 1.0, 0.0) for t in range(tiles)],
    ]
    for m in range(2):
        picked = [jnp.where(lane == row + 8 * t, left[m][t], 0.0) for t in range(tiles)]
        across = jnp.sum(functools.reduce(jnp.add, picked), axis=0, keepdims=True)
        across = 1.0 / jnp.sqrt(jnp.where(lane[0:1] < modes, across, 1.0))
        for t in range(tiles):
            down = 1.0 / jnp.sqrt(jnp.sum(picked[t], axis=1, keepdims=True))
            left[m][t] = left[m][t] * down * across
            right[m][t] = right[m][t] * down

    def spread_row(value, i):
        return jnp.broadcast_to(value[i : i + 1, :], (8, width))

    def spread_lane(value, k):
        return jnp.broadcast_to(value[:, k : k + 1], (8, width))

    done = [[None] * tiles, [None] * tiles]
    for k in range(0, modes, 4):
        home, sub = divmod(k, 8)
        near = [[spread_lane(left[m][home], k + j) for j in range(4)] for m in range(2)]
        steps = []
        for m in range(2):
            e = {(i, j): spread_row(near[m][j], sub + i) for j in range(4) for i in range(j, 4)}
            scale = 1.0 / (e[0, 0] * e[1, 1] - e[1, 0] * e[1, 0])
            r, q, p = e[1, 1] * scale, e[1, 0] * scale, e[0, 0] * scale
            u2, v2 = r * e[2, 0] - q * e[2, 1], p * e[2, 1] - q * e[2, 0]
            u3, v3 = r * e[3, 0] - q * e[3, 1], p * e[3, 1] - q * e[3, 0]
            s22 = e[2, 2] - (e[2, 0] * u2 + e[2, 1] * v2)
            s32 = e[3, 2] - (e[3, 0] * u2 + e[3, 1] * v2)
            s33 = e[3, 3] - (e[3, 0] * u3 + e[3, 1] * v3)
            scale = 1.0 / (s22 * s33 - s32 * s32)
            rr, qq, pp = s33 * scale, s32 * scale, s22 * scale
            found = []
            for value in (left[m][home], right[m][home]):
                g0, g1, g2, g3 = (spread_row(value, sub + i) for i in range(4))
                h2, h3 = g2 - (u2 * g0 + v2 * g1), g3 - (u3 * g0 + v3 * g1)
                x2, x3 = rr * h2 - qq * h3, pp * h3 - qq * h2
                x0 = (r * g0 - q * g1) - (u2 * x2 + u3 * x3)
                x1 = (p * g1 - q * g0) - (v2 * x2 + v3 * x3)
                found.append((x0, x1, x2, x3))
            steps.append(found)
            flat, flat2 = 1.0 / e[0, 0], 1.0 / s22
            ratio, ratio2 = e[1, 0] * flat, s32 * flat2
            y0, y1 = g0 * jnp.sqrt(flat), (g1 - ratio * g0) / jnp.sqrt(e[1, 1] - ratio * e[1, 0])
            y2, y3 = h2 * jnp.sqrt(flat2), (h3 - ratio2 * h2) / jnp.sqrt(s33 - ratio2 * s32)
            rows = jnp.where(
                row < sub + 2, jnp.where(row == sub, y0, y1), jnp.where(row == sub + 2, y2, y3)
            )
            done[m][home] = rows if sub == 0 else jnp.where(row >= sub, rows, done[m][home])
        for t in range(home, tiles):
            for m in range(2):
                if t > home:
                    f = [spread_lane(left[m][t], k + j) for j in range(4)]
                elif sub == 0:
                    f = [jnp.where(row > 3, part, 0.0) for part in near[m]]
                else:
                    continue
                for side, x in zip((left[m], right[m]), steps[m]):
                    side[t] = side[t] - ((f[0] * x[0] + f[1] * x[1]) + (f[2] * x[2] + f[3] * x[3]))

    basis_ref[...] = jnp.concatenate(done[0], axis=0)
    inverse = jnp.concatenate(done[1], axis=0)[:, 0:modes]
    cross = jnp.concatenate([tile(1, t) for t in range(tiles)], axis=0)[:, 0:modes]
    half = jnp.dot(inverse, cross, precision=HIGHEST, preferred_element_type=jnp.float32)
    ritz_ref[...] = nt_dot(half, inverse)


def call(kernel, out_shape, *args):
    return pl.pallas_call(kernel, out_shape=out_shape, compiler_params=PARAMS)(*args)


def body(node_coords, inv_range, mode_block):
    modes, width = mode_block.shape
    near_axes, far_axes, last = ("xl", "zl", "yl"), ("zh", "yh"), "xh"
    count = {axis: lax.axis_size(axis) for axis in near_axes + far_axes + (last, "c")}
    dests, sources = (math.prod(count[axis] for axis in axes) for axes in (near_axes, far_axes))
    node_total = math.prod(count.values()) * width
    row_send = call(row_kernel, jax.ShapeDtypeStruct((2 * dests, 16, width), jnp.bfloat16), node_coords)
    row_pack = lax.all_to_all(row_send, near_axes + ("c",), 0, 0)
    vmem = pl.BlockSpec(memory_space=pltpu.VMEM)
    block, weight = pl.pallas_call(
        block_kernel,
        out_shape=(
            jax.ShapeDtypeStruct((sources, modes + 16, width), jnp.bfloat16),
            jax.ShapeDtypeStruct((8, width), jnp.float32),
        ),
        in_specs=[pl.BlockSpec(memory_space=pltpu.SMEM), vmem, vmem],
        compiler_params=PARAMS,
    )(inv_range, row_send, mode_block)
    block, row_pack = lax.optimization_barrier((block, row_pack))
    block = lax.all_to_all(block, far_axes, 0, 0)
    other = lax.ppermute(block, last, [(0, 1), (1, 0)])
    core = lax.axis_index("c").astype(jnp.int32)[None]
    shared = functools.partial(covariance_part, core, weight, row_pack)
    far, near = shared(block, (1, 0))
    (far,) = shared(other, (1,), (far,))
    far = lax.ppermute(far, "c", [(0, 1), (1, 0)])
    (near,) = shared(other, (0,), (near,))
    pieces = lax.all_to_all(near + far, near_axes, 0, 0)
    split_axes = (last,) + near_axes + ("c",)
    slots = math.prod(count[axis] for axis in split_axes)
    levels = -(-2 * (modes // 8) // slots)
    image, grams = call(
        gram_kernel,
        (
            jax.ShapeDtypeStruct((modes, width), jnp.float32),
            jax.ShapeDtypeStruct((slots, 8 * levels, width), jnp.float32),
        ),
        pieces,
        mode_block,
    )
    for axes, copies in ((split_axes, sources), (far_axes, slots)):
        grams = lax.all_to_all(grams, axes, 0, 0)
        grams = call(spread_kernel, jax.ShapeDtypeStruct((copies, 8 * levels, width), jnp.float32), grams)
    grams = lax.all_to_all(grams, split_axes, 0, 0)
    basis, ritz = call(
        functools.partial(final_kernel, node_total),
        (
            jax.ShapeDtypeStruct((modes, width), jnp.float32),
            jax.ShapeDtypeStruct((modes, modes), jnp.float32),
        ),
        grams,
        image,
    )
    return (basis, ritz)


def solution(mesh):
    axes = ("xh", "xl", "zh", "zl", "yh", "yl", "c")
    parts = Mesh(mesh.devices.reshape(2, 2, 4, 2, 4, 2, 2), axes)
    nodes = P(None, axes)
    return jax.shard_map(
        body, mesh=parts, in_specs=(nodes, P(), nodes), out_specs=(nodes, P()), check_vma=False
    )
```

```python
import functools
import math

import jax
import jax.numpy as jnp
from jax import lax
from jax.experimental import pallas as pl
from jax.experimental.pallas import tpu as pltpu
from jax.sharding import Mesh, PartitionSpec as P

NUGGET = 0.25
LOG2E = math.log2(math.e)
HIGHEST = lax.Precision.HIGHEST
PARAMS = pltpu.CompilerParams(vmem_limit_bytes=48 * 1024 * 1024)


def scale_rows(range_ref):
    index = lax.broadcasted_iota(jnp.int32, (8, 128), 0)
    picked = jnp.where(
        index == 0,
        range_ref[0],
        jnp.where(index == 1, range_ref[1], jnp.where(index == 2, range_ref[2], 0.0)),
    )
    return picked * LOG2E


def split(pack, centre):
    parts = pack.astype(jnp.float32)
    return (parts[0:8] - centre) * 4.0, parts[8:16]


def halves_of(coords):
    coords = coords.astype(jnp.float32)
    if coords.shape[0] < 8:
        coords = jnp.concatenate([coords, jnp.zeros((8 - coords.shape[0], coords.shape[1]), jnp.float32)], axis=0)
    high = jnp.floor(coords * 0.25)
    return high, coords - 4.0 * high


def three_parts(value):
    one = value.astype(jnp.bfloat16).astype(jnp.float32)
    two = (value - one).astype(jnp.bfloat16).astype(jnp.float32)
    return [one, two, value - one - two]


def cov_kernel(halves, modes, core_ref, weight_ref, row_ref, col_ref, *refs):
    count = len(halves)
    start_refs, refs = refs[: len(refs) - 2 - count], refs[len(refs) - 2 - count :]
    out_refs, (rows, cols) = refs[:count], refs[count:]
    pieces, _, width = col_ref.shape
    dests = row_ref.shape[0] // 2
    weight = weight_ref[...]
    ones, blank = jnp.ones((1, width), jnp.float32), jnp.zeros((8, width), jnp.float32)
    total = sum(halves_of(row_ref[k])[0] for k in range(2 * dests))
    centre = jnp.round(jnp.sum(total, axis=1, keepdims=True) * (1.0 / (2 * dests * width)))
    low = jnp.concatenate([col_ref[piece, 0:modes, :] for piece in range(pieces)], axis=1)
    for piece in range(pieces):
        high, rest = split(col_ref[piece, modes : modes + 16, :], centre)
        norm = jnp.sum(weight * (high + rest) * (high + rest), axis=0, keepdims=True)
        norms = jnp.concatenate([ones] * 3 + three_parts(norm) + [blank[0:2]], axis=0)
        features = jnp.concatenate([high] * 3 + [rest] * 3 + [norms, blank], axis=0)
        cols[piece * width : (piece + 1) * width, :] = features.T.astype(jnp.bfloat16)
    for which, half in enumerate(halves):
        core = core_ref[0] if half == 0 else 1 - core_ref[0]
        for y in range(dests):
            high, rest = halves_of(row_ref[2 * y + core])
            place = (high - centre) * 4.0 + rest
            norm = jnp.sum(weight * place * place, axis=0, keepdims=True) + LOG2E * LOG2E
            norms = jnp.concatenate(three_parts(norm) + [ones] * 3 + [blank[0:2]], axis=0)
            cross = three_parts(-2.0 * weight * place)
            features = jnp.concatenate(cross + cross + [norms, blank], axis=0)
            rows[which, :, y * width : (y + 1) * width] = features.astype(jnp.bfloat16)
        group = 4
        for first in range(0, dests, group):
            span = slice(first * width, (first + group) * width)
            total = jnp.dot(cols[...], rows[which, :, span], preferred_element_type=jnp.float32)
            total = jnp.maximum(total, LOG2E * LOG2E)
            cov = jnp.exp2(LOG2E - total * lax.rsqrt(total)).astype(jnp.bfloat16)
            update = jnp.dot(low, cov, preferred_element_type=jnp.float32)
            for y in range(group):
                term = update[:, y * width : (y + 1) * width]
                if start_refs:
                    term = term + start_refs[which][first + y]
                out_refs[which][first + y] = term


def covariance_part(core, weight, row_pack, col_pack, halves, starts=()):
    dests, _, width = row_pack.shape
    dests = dests // 2
    modes = col_pack.shape[1] - 16
    pairs = col_pack.shape[0] * dests * width * width * len(halves)
    vmem = pl.BlockSpec(memory_space=pltpu.VMEM)
    smem = pl.BlockSpec(memory_space=pltpu.SMEM)
    args = (core, weight, row_pack, col_pack) + tuple(starts)
    return pl.pallas_call(
        functools.partial(cov_kernel, halves, modes),
        out_shape=[jax.ShapeDtypeStruct((dests, modes, width), jnp.float32)] * len(halves),
        in_specs=[smem] + [vmem] * (len(args) - 1),
        out_specs=[vmem] * len(halves),
        scratch_shapes=[
            pltpu.VMEM((len(halves), 64, dests * width), jnp.bfloat16),
            pltpu.VMEM((col_pack.shape[0] * width, 64), jnp.bfloat16),
        ],
        input_output_aliases={4 + k: k for k in range(len(starts))},
        compiler_params=PARAMS,
        cost_estimate=pl.CostEstimate(
            flops=pairs * 2 * modes * 4, bytes_accessed=4 * dests * modes * width, transcendentals=2 * pairs
        ),
    )(*args)


def nt_dot(left, right):
    return lax.dot_general(
        left, right, (((1,), (1,)), ((), ())), precision=HIGHEST, preferred_element_type=jnp.float32
    )


def block_kernel(range_ref, coord_ref, mode_ref, out_ref, weight_ref):
    scale = scale_rows(range_ref)
    weight_ref[...] = scale * scale
    coords = jnp.concatenate(halves_of(coord_ref[...]), axis=0).astype(jnp.bfloat16)
    pack = jnp.concatenate([mode_ref[...].astype(jnp.bfloat16), coords], axis=0)
    for k in range(out_ref.shape[0]):
        out_ref[k] = pack


def gram_kernel(part_ref, mode_ref, image_ref, gram_ref):
    image = part_ref[0]
    for y in range(1, part_ref.shape[0]):
        image = image + part_ref[y]
    mode = mode_ref[...]
    image = image + NUGGET * mode
    image_ref[...] = image
    modes, width = image.shape
    third = modes // 3
    blank = jnp.zeros((third, width), jnp.float32)
    one, two = mode[third : 2 * third], mode[2 * third :]
    left = jnp.concatenate(
        [image, jnp.concatenate([one, two, blank], axis=0), jnp.concatenate([blank, blank, two], axis=0)], axis=1
    )
    right = jnp.concatenate(
        [
            jnp.concatenate([image, jnp.zeros((modes, 2 * width), jnp.float32)], axis=1),
            jnp.concatenate([blank, one, two], axis=1),
        ],
        axis=0,
    )
    grams = (nt_dot(left, right), nt_dot(mode, jnp.concatenate([image, mode[:third]], axis=0)))
    tiles, slots = modes // 8, gram_ref.shape[0]
    for slot in range(2 * tiles % slots, slots):
        gram_ref[slot, gram_ref.shape[1] - 8 :, :] = jnp.zeros((8, width), jnp.float32)
    for which, gram in enumerate(grams):
        for t in range(tiles):
            level, slot = divmod(which * tiles + t, slots)
            gram_ref[slot, level * 8 : level * 8 + 8, :] = gram[t * 8 : t * 8 + 8, :]


def spread_kernel(part_ref, out_ref):
    total = part_ref[0]
    for k in range(1, part_ref.shape[0]):
        total = total + part_ref[k]
    for k in range(out_ref.shape[0]):
        out_ref[k] = total


def final_kernel(node_total, gram_ref, image_ref, basis_ref, ritz_ref):
    modes, width = image_ref.shape
    tiles = modes // 8
    slots = gram_ref.shape[0]

    def tile(which, t):
        level, slot = divmod(which * tiles + t, slots)
        return gram_ref[slot, level * 8 : level * 8 + 8, :] * (1.0 / node_total)

    lane = lax.broadcasted_iota(jnp.int32, (8, width), 1)
    row = lax.broadcasted_iota(jnp.int32, (8, width), 0)
    third = modes // 3
    lower = []
    for t in range(tiles):
        block = 8 * t // third
        value = pltpu.roll(tile(1, t), third, 1)
        if block >= 1:
            moved = pltpu.roll(tile(0, t - third // 8), 2 * third, 1)
            value = jnp.where(lane < third, value, moved)
        if block == 2:
            moved = pltpu.roll(tile(0, t), 3 * third, 1)
            value = jnp.where(lane < 2 * third, value, moved)
        lower.append(jnp.where(lane < (block + 1) * third, value, 0.0))
    upper = jnp.concatenate(lower + [jnp.zeros((width - modes, width), jnp.float32)], axis=0).T
    left = [
        [tile(0, t) for t in range(tiles)],
        [
            jnp.where(lane < (8 * t // third + 1) * third, lower[t], upper[8 * t : 8 * t + 8, :])
            for t in range(tiles)
        ],
    ]
    right = [
        [image_ref[t * 8 : t * 8 + 8, :] for t in range(tiles)],
        [jnp.where(lane == row + 8 * t, 1.0, 0.0) for t in range(tiles)],
    ]
    for m in range(2):
        picked = [jnp.where(lane == row + 8 * t, left[m][t], 0.0) for t in range(tiles)]
        across = jnp.sum(functools.reduce(jnp.add, picked), axis=0, keepdims=True)
        across = 1.0 / jnp.sqrt(jnp.where(lane[0:1] < modes, across, 1.0))
        for t in range(tiles):
            down = 1.0 / jnp.sqrt(jnp.sum(picked[t], axis=1, keepdims=True))
            left[m][t] = left[m][t] * down * across
            right[m][t] = right[m][t] * down

    def spread_row(value, i):
        return jnp.broadcast_to(value[i : i + 1, :], (8, width))

    def spread_lane(value, k):
        return jnp.broadcast_to(value[:, k : k + 1], (8, width))

    done = [[None] * tiles, [None] * tiles]
    for k in range(0, modes, 4):
        home, sub = divmod(k, 8)
        near = [[spread_lane(left[m][home], k + j) for j in range(4)] for m in range(2)]
        steps = []
        for m in range(2):
            e = {(i, j): spread_row(near[m][j], sub + i) for j in range(4) for i in range(j, 4)}
            scale = 1.0 / (e[0, 0] * e[1, 1] - e[1, 0] * e[1, 0])
            r, q, p = e[1, 1] * scale, e[1, 0] * scale, e[0, 0] * scale
            u2, v2 = r * e[2, 0] - q * e[2, 1], p * e[2, 1] - q * e[2, 0]
            u3, v3 = r * e[3, 0] - q * e[3, 1], p * e[3, 1] - q * e[3, 0]
            s22 = e[2, 2] - (e[2, 0] * u2 + e[2, 1] * v2)
            s32 = e[3, 2] - (e[3, 0] * u2 + e[3, 1] * v2)
            s33 = e[3, 3] - (e[3, 0] * u3 + e[3, 1] * v3)
            scale = 1.0 / (s22 * s33 - s32 * s32)
            rr, qq, pp = s33 * scale, s32 * scale, s22 * scale
            found = []
            for value in (left[m][home], right[m][home]):
                g0, g1, g2, g3 = (spread_row(value, sub + i) for i in range(4))
                h2, h3 = g2 - (u2 * g0 + v2 * g1), g3 - (u3 * g0 + v3 * g1)
                x2, x3 = rr * h2 - qq * h3, pp * h3 - qq * h2
                x0 = (r * g0 - q * g1) - (u2 * x2 + u3 * x3)
                x1 = (p * g1 - q * g0) - (v2 * x2 + v3 * x3)
                found.append((x0, x1, x2, x3))
            steps.append(found)
            flat, flat2 = 1.0 / e[0, 0], 1.0 / s22
            ratio, ratio2 = e[1, 0] * flat, s32 * flat2
            y0, y1 = g0 * jnp.sqrt(flat), (g1 - ratio * g0) / jnp.sqrt(e[1, 1] - ratio * e[1, 0])
            y2, y3 = h2 * jnp.sqrt(flat2), (h3 - ratio2 * h2) / jnp.sqrt(s33 - ratio2 * s32)
            rows = jnp.where(
                row < sub + 2, jnp.where(row == sub, y0, y1), jnp.where(row == sub + 2, y2, y3)
            )
            done[m][home] = rows if sub == 0 else jnp.where(row >= sub, rows, done[m][home])
        for t in range(home, tiles):
            for m in range(2):
                if t > home:
                    f = [spread_lane(left[m][t], k + j) for j in range(4)]
                elif sub == 0:
                    f = [jnp.where(row > 3, part, 0.0) for part in near[m]]
                else:
                    continue
                for side, x in zip((left[m], right[m]), steps[m]):
                    side[t] = side[t] - ((f[0] * x[0] + f[1] * x[1]) + (f[2] * x[2] + f[3] * x[3]))

    basis_ref[...] = jnp.concatenate(done[0], axis=0)
    inverse = jnp.concatenate(done[1], axis=0)[:, 0:modes]
    cross = jnp.concatenate([tile(1, t) for t in range(tiles)], axis=0)[:, 0:modes]
    half = jnp.dot(inverse, cross, precision=HIGHEST, preferred_element_type=jnp.float32)
    ritz_ref[...] = nt_dot(half, inverse)


def call(kernel, out_shape, *args):
    return pl.pallas_call(kernel, out_shape=out_shape, compiler_params=PARAMS)(*args)


def body(node_coords, inv_range, mode_block):
    modes, width = mode_block.shape
    near_axes, far_axes, last = ("xh", "zl", "yl"), ("zh", "yh"), "xl"
    count = {axis: lax.axis_size(axis) for axis in near_axes + far_axes + (last, "c")}
    dests, sources = (math.prod(count[axis] for axis in axes) for axes in (near_axes, far_axes))
    node_total = math.prod(count.values()) * width
    row_send = jnp.pad(node_coords, ((0, 8 - node_coords.shape[0]), (0, 0)))
    row_send = jnp.broadcast_to(row_send[None], (2 * dests,) + row_send.shape)
    row_pack = lax.all_to_all(row_send, near_axes + ("c",), 0, 0)
    vmem = pl.BlockSpec(memory_space=pltpu.VMEM)
    block, weight = pl.pallas_call(
        block_kernel,
        out_shape=(
            jax.ShapeDtypeStruct((sources, modes + 16, width), jnp.bfloat16),
            jax.ShapeDtypeStruct((8, width), jnp.float32),
        ),
        in_specs=[pl.BlockSpec(memory_space=pltpu.SMEM), vmem, vmem],
        compiler_params=PARAMS,
    )(inv_range, node_coords, mode_block)
    block, row_pack = lax.optimization_barrier((block, row_pack))
    block = lax.all_to_all(block, far_axes, 0, 0)
    other = lax.ppermute(block, last, [(0, 1), (1, 0)])
    core = lax.axis_index("c").astype(jnp.int32)[None]
    shared = functools.partial(covariance_part, core, weight, row_pack)
    far, near = shared(block, (1, 0))
    (far,) = shared(other, (1,), (far,))
    far = lax.ppermute(far, "c", [(0, 1), (1, 0)])
    (near,) = shared(other, (0,), (near,))
    pieces = lax.all_to_all(near + far, near_axes, 0, 0)
    split_axes, joint_axes = (last,) + near_axes + ("c",), far_axes
    slots, joined = (math.prod(count[axis] for axis in axes) for axes in (split_axes, joint_axes))
    levels = -(-2 * (modes // 8) // slots)
    image, grams = call(
        gram_kernel,
        (
            jax.ShapeDtypeStruct((modes, width), jnp.float32),
            jax.ShapeDtypeStruct((slots, 8 * levels, width), jnp.float32),
        ),
        pieces,
        mode_block,
    )
    for axes, copies in ((split_axes, joined), (joint_axes, slots)):
        grams = lax.all_to_all(grams, axes, 0, 0)
        grams = call(spread_kernel, jax.ShapeDtypeStruct((copies, 8 * levels, width), jnp.float32), grams)
    grams = lax.all_to_all(grams, split_axes, 0, 0)
    basis, ritz = call(
        functools.partial(final_kernel, node_total),
        (
            jax.ShapeDtypeStruct((modes, width), jnp.float32),
            jax.ShapeDtypeStruct((modes, modes), jnp.float32),
        ),
        grams,
        image,
    )
    return (basis, ritz)


def solution(mesh):
    axes = ("xh", "xl", "zh", "zl", "yh", "yl", "c")
    parts = Mesh(mesh.devices.reshape(2, 2, 4, 2, 4, 2, 2), axes)
    nodes = P(None, axes)
    return jax.shard_map(
        body, mesh=parts, in_specs=(nodes, P(), nodes), out_specs=(nodes, P()), check_vma=False
    )
```

```python
import functools
import math

import jax
import jax.numpy as jnp
from jax import lax
from jax.experimental import pallas as pl
from jax.experimental.pallas import tpu as pltpu
from jax.sharding import Mesh, PartitionSpec as P

NUGGET = 0.25
LOG2E = math.log2(math.e)
HIGHEST = lax.Precision.HIGHEST
PARAMS = pltpu.CompilerParams(vmem_limit_bytes=48 * 1024 * 1024)


def scale_rows(range_ref):
    index = lax.broadcasted_iota(jnp.int32, (8, 128), 0)
    picked = jnp.where(
        index == 0,
        range_ref[0],
        jnp.where(index == 1, range_ref[1], jnp.where(index == 2, range_ref[2], 0.0)),
    )
    return picked * LOG2E


def split(pack, centre):
    parts = pack.astype(jnp.float32)
    return (parts[0:8] - centre) * 4.0, parts[8:16]


def halves_of(coords):
    coords = coords.astype(jnp.float32)
    coords = jnp.concatenate([coords, jnp.zeros((8 - coords.shape[0], coords.shape[1]), jnp.float32)], axis=0)
    high = jnp.floor(coords * 0.25)
    return high, coords - 4.0 * high


def three_parts(value):
    one = value.astype(jnp.bfloat16).astype(jnp.float32)
    two = (value - one).astype(jnp.bfloat16).astype(jnp.float32)
    return [one, two, value - one - two]


def cov_kernel(halves, modes, core_ref, weight_ref, row_ref, col_ref, *refs):
    count = len(halves)
    start_refs, refs = refs[: len(refs) - 2 - count], refs[len(refs) - 2 - count :]
    out_refs, (rows, cols) = refs[:count], refs[count:]
    pieces, _, width = col_ref.shape
    dests = row_ref.shape[0] // 2
    weight = weight_ref[...]
    ones, blank = jnp.ones((1, width), jnp.float32), jnp.zeros((8, width), jnp.float32)
    total = sum(halves_of(row_ref[k])[0] for k in range(2 * dests))
    centre = jnp.round(jnp.sum(total, axis=1, keepdims=True) * (1.0 / (2 * dests * width)))
    low = jnp.concatenate([col_ref[piece, 0:modes, :] for piece in range(pieces)], axis=1)
    for piece in range(pieces):
        high, rest = split(col_ref[piece, modes : modes + 16, :], centre)
        norm = jnp.sum(weight * (high + rest) * (high + rest), axis=0, keepdims=True)
        norms = jnp.concatenate([ones] * 3 + three_parts(norm) + [blank[0:2]], axis=0)
        features = jnp.concatenate([high] * 3 + [rest] * 3 + [norms, blank], axis=0)
        cols[piece * width : (piece + 1) * width, :] = features.T.astype(jnp.bfloat16)
    for which, half in enumerate(halves):
        core = core_ref[0] if half == 0 else 1 - core_ref[0]
        for y in range(dests):
            high, rest = halves_of(row_ref[2 * y + core])
            place = (high - centre) * 4.0 + rest
            norm = jnp.sum(weight * place * place, axis=0, keepdims=True) + LOG2E * LOG2E
            norms = jnp.concatenate(three_parts(norm) + [ones] * 3 + [blank[0:2]], axis=0)
            cross = three_parts(-2.0 * weight * place)
            features = jnp.concatenate(cross + cross + [norms, blank], axis=0)
            rows[which, :, y * width : (y + 1) * width] = features.astype(jnp.bfloat16)
        group = dests
        for first in range(0, dests, group):
            span = slice(first * width, (first + group) * width)
            total = jnp.dot(cols[...], rows[which, :, span], preferred_element_type=jnp.float32)
            total = jnp.maximum(total, LOG2E * LOG2E)
            cov = jnp.exp2(LOG2E - total * lax.rsqrt(total)).astype(jnp.bfloat16)
            update = jnp.dot(low, cov, preferred_element_type=jnp.float32)
            for y in range(group):
                term = update[:, y * width : (y + 1) * width]
                if start_refs:
                    term = term + start_refs[which][first + y]
                out_refs[which][first + y] = term


def covariance_part(core, weight, row_pack, col_pack, halves, starts=()):
    dests, _, width = row_pack.shape
    dests = dests // 2
    modes = col_pack.shape[1] - 16
    pairs = col_pack.shape[0] * dests * width * width * len(halves)
    vmem = pl.BlockSpec(memory_space=pltpu.VMEM)
    smem = pl.BlockSpec(memory_space=pltpu.SMEM)
    args = (core, weight, row_pack, col_pack) + tuple(starts)
    return pl.pallas_call(
        functools.partial(cov_kernel, halves, modes),
        out_shape=[jax.ShapeDtypeStruct((dests, modes, width), jnp.float32)] * len(halves),
        in_specs=[smem] + [vmem] * (len(args) - 1),
        out_specs=[vmem] * len(halves),
        scratch_shapes=[
            pltpu.VMEM((len(halves), 64, dests * width), jnp.bfloat16),
            pltpu.VMEM((col_pack.shape[0] * width, 64), jnp.bfloat16),
        ],
        input_output_aliases={4 + k: k for k in range(len(starts))},
        compiler_params=PARAMS,
        cost_estimate=pl.CostEstimate(
            flops=pairs * 2 * modes * 4, bytes_accessed=4 * dests * modes * width, transcendentals=2 * pairs
        ),
    )(*args)


def nt_dot(left, right):
    return lax.dot_general(
        left, right, (((1,), (1,)), ((), ())), precision=HIGHEST, preferred_element_type=jnp.float32
    )


def block_kernel(range_ref, coord_ref, mode_ref, out_ref, weight_ref):
    scale = scale_rows(range_ref)
    weight_ref[...] = scale * scale
    coords = jnp.concatenate(halves_of(coord_ref[...]), axis=0).astype(jnp.bfloat16)
    pack = jnp.concatenate([mode_ref[...].astype(jnp.bfloat16), coords], axis=0)
    for k in range(out_ref.shape[0]):
        out_ref[k] = pack


def gram_kernel(part_ref, mode_ref, image_ref, gram_ref):
    image = part_ref[0]
    for y in range(1, part_ref.shape[0]):
        image = image + part_ref[y]
    mode = mode_ref[...]
    image = image + NUGGET * mode
    image_ref[...] = image
    modes, width = image.shape
    third = modes // 3
    blank = jnp.zeros((third, width), jnp.float32)
    one, two = mode[third : 2 * third], mode[2 * third :]
    left = jnp.concatenate(
        [image, jnp.concatenate([one, two, blank], axis=0), jnp.concatenate([blank, blank, two], axis=0)], axis=1
    )
    right = jnp.concatenate(
        [
            jnp.concatenate([image, jnp.zeros((modes, 2 * width), jnp.float32)], axis=1),
            jnp.concatenate([blank, one, two], axis=1),
        ],
        axis=0,
    )
    grams = (nt_dot(left, right), nt_dot(mode, jnp.concatenate([image, mode[:third]], axis=0)))
    tiles, slots = modes // 8, gram_ref.shape[0]
    for slot in range(2 * tiles % slots, slots):
        gram_ref[slot, gram_ref.shape[1] - 8 :, :] = jnp.zeros((8, width), jnp.float32)
    for which, gram in enumerate(grams):
        for t in range(tiles):
            level, slot = divmod(which * tiles + t, slots)
            gram_ref[slot, level * 8 : level * 8 + 8, :] = gram[t * 8 : t * 8 + 8, :]


def spread_kernel(part_ref, out_ref):
    total = part_ref[0]
    for k in range(1, part_ref.shape[0]):
        total = total + part_ref[k]
    for k in range(out_ref.shape[0]):
        out_ref[k] = total


def final_kernel(node_total, gram_ref, image_ref, basis_ref, ritz_ref):
    modes, width = image_ref.shape
    tiles = modes // 8
    slots = gram_ref.shape[0]

    def tile(which, t):
        level, slot = divmod(which * tiles + t, slots)
        return gram_ref[slot, level * 8 : level * 8 + 8, :] * (1.0 / node_total)

    lane = lax.broadcasted_iota(jnp.int32, (8, width), 1)
    row = lax.broadcasted_iota(jnp.int32, (8, width), 0)
    third = modes // 3
    lower = []
    for t in range(tiles):
        block = 8 * t // third
        value = pltpu.roll(tile(1, t), third, 1)
        if block >= 1:
            moved = pltpu.roll(tile(0, t - third // 8), 2 * third, 1)
            value = jnp.where(lane < third, value, moved)
        if block == 2:
            moved = pltpu.roll(tile(0, t), 3 * third, 1)
            value = jnp.where(lane < 2 * third, value, moved)
        lower.append(jnp.where(lane < (block + 1) * third, value, 0.0))
    upper = jnp.concatenate(lower + [jnp.zeros((width - modes, width), jnp.float32)], axis=0).T
    left = [
        [tile(0, t) for t in range(tiles)],
        [
            jnp.where(lane < (8 * t // third + 1) * third, lower[t], upper[8 * t : 8 * t + 8, :])
            for t in range(tiles)
        ],
    ]
    right = [
        [image_ref[t * 8 : t * 8 + 8, :] for t in range(tiles)],
        [jnp.where(lane == row + 8 * t, 1.0, 0.0) for t in range(tiles)],
    ]
    for m in range(2):
        picked = [jnp.where(lane == row + 8 * t, left[m][t], 0.0) for t in range(tiles)]
        across = jnp.sum(functools.reduce(jnp.add, picked), axis=0, keepdims=True)
        across = 1.0 / jnp.sqrt(jnp.where(lane[0:1] < modes, across, 1.0))
        for t in range(tiles):
            down = 1.0 / jnp.sqrt(jnp.sum(picked[t], axis=1, keepdims=True))
            left[m][t] = left[m][t] * down * across
            right[m][t] = right[m][t] * down

    def spread_row(value, i):
        return jnp.broadcast_to(value[i : i + 1, :], (8, width))

    def spread_lane(value, k):
        return jnp.broadcast_to(value[:, k : k + 1], (8, width))

    done = [[None] * tiles, [None] * tiles]
    for k in range(0, modes, 4):
        home, sub = divmod(k, 8)
        near = [[spread_lane(left[m][home], k + j) for j in range(4)] for m in range(2)]
        steps = []
        for m in range(2):
            e = {(i, j): spread_row(near[m][j], sub + i) for j in range(4) for i in range(j, 4)}
            scale = 1.0 / (e[0, 0] * e[1, 1] - e[1, 0] * e[1, 0])
            r, q, p = e[1, 1] * scale, e[1, 0] * scale, e[0, 0] * scale
            u2, v2 = r * e[2, 0] - q * e[2, 1], p * e[2, 1] - q * e[2, 0]
            u3, v3 = r * e[3, 0] - q * e[3, 1], p * e[3, 1] - q * e[3, 0]
            s22 = e[2, 2] - (e[2, 0] * u2 + e[2, 1] * v2)
            s32 = e[3, 2] - (e[3, 0] * u2 + e[3, 1] * v2)
            s33 = e[3, 3] - (e[3, 0] * u3 + e[3, 1] * v3)
            scale = 1.0 / (s22 * s33 - s32 * s32)
            rr, qq, pp = s33 * scale, s32 * scale, s22 * scale
            found = []
            for value in (left[m][home], right[m][home]):
                g0, g1, g2, g3 = (spread_row(value, sub + i) for i in range(4))
                h2, h3 = g2 - (u2 * g0 + v2 * g1), g3 - (u3 * g0 + v3 * g1)
                x2, x3 = rr * h2 - qq * h3, pp * h3 - qq * h2
                x0 = (r * g0 - q * g1) - (u2 * x2 + u3 * x3)
                x1 = (p * g1 - q * g0) - (v2 * x2 + v3 * x3)
                found.append((x0, x1, x2, x3))
            steps.append(found)
            flat, flat2 = 1.0 / e[0, 0], 1.0 / s22
            ratio, ratio2 = e[1, 0] * flat, s32 * flat2
            y0, y1 = g0 * jnp.sqrt(flat), (g1 - ratio * g0) / jnp.sqrt(e[1, 1] - ratio * e[1, 0])
            y2, y3 = h2 * jnp.sqrt(flat2), (h3 - ratio2 * h2) / jnp.sqrt(s33 - ratio2 * s32)
            rows = jnp.where(
                row < sub + 2, jnp.where(row == sub, y0, y1), jnp.where(row == sub + 2, y2, y3)
            )
            done[m][home] = rows if sub == 0 else jnp.where(row >= sub, rows, done[m][home])
        for t in range(home, tiles):
            for m in range(2):
                if t > home:
                    f = [spread_lane(left[m][t], k + j) for j in range(4)]
                elif sub == 0:
                    f = [jnp.where(row > 3, part, 0.0) for part in near[m]]
                else:
                    continue
                for side, x in zip((left[m], right[m]), steps[m]):
                    side[t] = side[t] - ((f[0] * x[0] + f[1] * x[1]) + (f[2] * x[2] + f[3] * x[3]))

    basis_ref[...] = jnp.concatenate(done[0], axis=0)
    inverse = jnp.concatenate(done[1], axis=0)[:, 0:modes]
    cross = jnp.concatenate([tile(1, t) for t in range(tiles)], axis=0)[:, 0:modes]
    half = jnp.dot(inverse, cross, precision=HIGHEST, preferred_element_type=jnp.float32)
    ritz_ref[...] = nt_dot(half, inverse)


def call(kernel, out_shape, *args):
    return pl.pallas_call(kernel, out_shape=out_shape, compiler_params=PARAMS)(*args)


def body(node_coords, inv_range, mode_block):
    modes, width = mode_block.shape
    near_axes, far_axes, last = ("xl", "zl", "yl"), ("zh", "yh"), "xh"
    count = {axis: lax.axis_size(axis) for axis in near_axes + far_axes + (last, "c")}
    dests, sources = (math.prod(count[axis] for axis in axes) for axes in (near_axes, far_axes))
    node_total = math.prod(count.values()) * width
    row_send = jnp.broadcast_to(node_coords[None], (2 * dests,) + node_coords.shape)
    row_pack = lax.all_to_all(row_send, near_axes + ("c",), 0, 0)
    vmem = pl.BlockSpec(memory_space=pltpu.VMEM)
    block, weight = pl.pallas_call(
        block_kernel,
        out_shape=(
            jax.ShapeDtypeStruct((sources, modes + 16, width), jnp.bfloat16),
            jax.ShapeDtypeStruct((8, width), jnp.float32),
        ),
        in_specs=[pl.BlockSpec(memory_space=pltpu.SMEM), vmem, vmem],
        compiler_params=PARAMS,
    )(inv_range, node_coords, mode_block)
    block, row_pack = lax.optimization_barrier((block, row_pack))
    block = lax.all_to_all(block, far_axes, 0, 0)
    other = lax.ppermute(block, last, [(0, 1), (1, 0)])
    core = lax.axis_index("c").astype(jnp.int32)[None]
    shared = functools.partial(covariance_part, core, weight, row_pack)
    far, near = shared(block, (1, 0))
    (far,) = shared(other, (1,), (far,))
    far = lax.ppermute(far, "c", [(0, 1), (1, 0)])
    (near,) = shared(other, (0,), (near,))
    pieces = lax.all_to_all(near + far, near_axes, 0, 0)
    split_axes, joint_axes = (last,) + near_axes + ("c",), far_axes
    slots, joined = (math.prod(count[axis] for axis in axes) for axes in (split_axes, joint_axes))
    levels = -(-2 * (modes // 8) // slots)
    image, grams = call(
        gram_kernel,
        (
            jax.ShapeDtypeStruct((modes, width), jnp.float32),
            jax.ShapeDtypeStruct((slots, 8 * levels, width), jnp.float32),
        ),
        pieces,
        mode_block,
    )
    for axes, copies in ((split_axes, joined), (joint_axes, slots)):
        grams = lax.all_to_all(grams, axes, 0, 0)
        grams = call(spread_kernel, jax.ShapeDtypeStruct((copies, 8 * levels, width), jnp.float32), grams)
    grams = lax.all_to_all(grams, split_axes, 0, 0)
    basis, ritz = call(
        functools.partial(final_kernel, node_total),
        (
            jax.ShapeDtypeStruct((modes, width), jnp.float32),
            jax.ShapeDtypeStruct((modes, modes), jnp.float32),
        ),
        grams,
        image,
    )
    return (basis, ritz)


def solution(mesh):
    axes = ("xh", "xl", "zh", "zl", "yh", "yl", "c")
    parts = Mesh(mesh.devices.reshape(2, 2, 4, 2, 4, 2, 2), axes)
    nodes = P(None, axes)
    return jax.shard_map(
        body, mesh=parts, in_specs=(nodes, P(), nodes), out_specs=(nodes, P()), check_vma=False
    )
```
